256 devices in a mesh: region: 8 (over x, core), dev: 32 (over z, y).
Axes of the slice: x: 4, y: 4, z: 8, core: 2. Of those that a mesh axis runs over, the one named last changes fastest.
Arguments:
- features: bfloat16 [64, 64, 256, 128], P(None, 'region', 'dev'), may hold values from -6 to 6
- occupancy: int32 [8, 32, 16], replicated, may hold values from 0 to 1
- weight_one: bfloat16 [64, 64, 3, 3, 3], replicated, may hold values from -0.15625 to 0.15625
- bias_one: float32 [64], replicated, may hold values from -3 to 3
- weight_two: bfloat16 [64, 64, 3, 3, 3], replicated, may hold values from -0.15625 to 0.15625
- bias_two: float32 [64], replicated, may hold values from -3 to 3
- weight_down: bfloat16 [64, 64, 2, 2, 2], replicated, may hold values from -0.25 to 0.25
- bias_down: float32 [64], replicated, may hold values from -3 to 3
Outputs:
- skip_maps: bfloat16 [64, 64, 256, 128], P(None, 'region', 'dev')
- down_maps: bfloat16 [64, 32, 8192], P(None, 'region', 'dev')
The draws below stay inside these ranges and needn't reach their ends.
All inputs are finite; a program needn't handle non-finite values.
Results may differ from the reference program's by a relative error of at most 0.0047.
Values may be sent and summed in bfloat16 or wider, within the bound.
A program may use at most 128 MiB of HBM per device.

```python
import jax
import jax.numpy as jnp
from jax import lax

C = 64
BR = 8
P_SIZE = 16
NX = 64
NY = 256
NZ = 128
N_REGION = 8
N_DEV = 32


def draw_occupancy(key, part):
    key = jax.random.fold_in(key, 11)
    first_key, second_key, third_key = jax.random.split(key, 3)
    base = jax.random.randint(first_key, (N_REGION, 1, 1), 1, 9)
    offset = jax.random.randint(second_key, (N_REGION, N_DEV, 1), -3, 4)
    level = jnp.clip(base + offset, 0, 8)
    rolled = jax.random.randint(third_key, (N_REGION, N_DEV, P_SIZE), 0, 8)
    return (rolled < level).astype(jnp.int32)


def block_scale(rng, dims, pieces, smallest, largest):
    level, own = 1.0, jax.random.fold_in(rng, 6)
    for dim, parts in pieces:
        steps = jnp.exp(jax.random.uniform(jax.random.fold_in(own, dim), (parts,), jnp.float32, smallest / len(pieces), largest / len(pieces)))
        level = level * jnp.repeat(steps, dims[dim] // parts).reshape([-1 if axis == dim else 1 for axis in range(len(dims))])
    return level


def noise(key, extent, deviation, reach, pieces=(), held_as=jnp.bfloat16):
    level = block_scale(key, extent, pieces, -0.22, 0.18) if pieces else 1.0
    values = jax.random.normal(key, extent, jnp.float32) * deviation * level
    return jnp.minimum(jnp.maximum(values, -reach), reach).astype(held_as)


def setup_inputs(seed: int = 0) -> dict:
    keys = jax.random.split(jax.random.key(seed), 9)
    return {
        "features": noise(keys[0], (C, NX, NY, NZ), 1.0, 6.0, ((1, 8), (2, 32))),
        "occupancy": draw_occupancy(jax.random.fold_in(keys[8], 71), 0),
        "weight_one": noise(keys[2], (C, C, 3, 3, 3), (C * 27) ** -0.5, 0.15625),
        "bias_one": noise(keys[3], (C,), 0.5, 3.0, (), jnp.float32),
        "weight_two": noise(keys[4], (C, C, 3, 3, 3), (C * 27) ** -0.5, 0.15625),
        "bias_two": noise(keys[5], (C,), 0.5, 3.0, (), jnp.float32),
        "weight_down": noise(keys[6], (C, C, 2, 2, 2), (C * 8) ** -0.5, 0.25),
        "bias_down": noise(keys[7], (C,), 0.5, 3.0, (), jnp.float32),
    }


def conv_layer(volume, weight, offset, edge_pad):
    summed = lax.conv_general_dilated(volume.astype(jnp.float32)[None], weight.astype(jnp.float32), (1, 1, 1), [(0, 0), (edge_pad, edge_pad), (edge_pad, edge_pad)], dimension_numbers=("NCDHW", "OIDHW", "NCDHW"), precision=lax.Precision.HIGHEST)[0]
    return jnp.maximum(summed + offset[:, None, None, None], 0.0)


def reference(features, occupancy, weight_one, bias_one, weight_two, bias_two, weight_down, bias_down):
    occupied = occupancy.astype(jnp.float32)
    mask = jnp.repeat(jnp.repeat(jnp.repeat(occupied, BR, 0), BR, 1), BR, 2)
    masked = jnp.where(mask[None] > 0, features, jnp.zeros_like(features))
    padded_input = jnp.pad(masked, ((0, 0), (2, 2), (0, 0), (0, 0)))
    padded_mask = jnp.pad(mask, ((2, 2), (0, 0), (0, 0)))

    def region_slab(region_number):
        start = (region_number * BR).astype(jnp.int32)
        slab = lax.dynamic_slice_in_dim(padded_input, start, BR + 4, 1)
        slab_mask = lax.dynamic_slice_in_dim(padded_mask, start, BR + 4, 0)
        first = (conv_layer(slab, weight_one, bias_one, 1) * slab_mask[1:-1][None]).astype(jnp.bfloat16)
        second = (conv_layer(first, weight_two, bias_two, 1) * slab_mask[2:-2][None]).astype(jnp.bfloat16)
        lowered = lax.conv_general_dilated(second.astype(jnp.float32)[None], weight_down.astype(jnp.float32), (2, 2, 2), "VALID", dimension_numbers=("NCDHW", "OIDHW", "NCDHW"), precision=lax.Precision.HIGHEST)[0]
        lowered = jnp.maximum(lowered + bias_down[:, None, None, None], 0.0).astype(jnp.bfloat16)
        return second, lowered

    seconds, lowereds = lax.map(region_slab, jnp.arange(N_REGION, dtype=jnp.int32))
    width = features.shape[0]
    skip_maps = jnp.transpose(seconds, (1, 0, 2, 3, 4)).reshape(width, NX, NY, NZ)
    down_maps = jnp.transpose(lowereds, (1, 0, 2, 3, 4)).reshape(width, NX // 2, NY * NZ // 4)
    return skip_maps, down_maps
```

```python
import functools

import jax
import jax.numpy as jnp
from jax import lax
from jax.experimental import pallas as pl
from jax.experimental.pallas import tpu as pltpu
from jax.sharding import PartitionSpec as P

MESH = pl.DeviceIdType.MESH
WAYS = ((0, 1), (0, -1), (1, 0), (-1, 0), (1, 1), (1, -1), (-1, 1), (-1, -1))
E = 8
C = 64
Z = 128
TAPS = 9


def source_span(step):
    return pl.ds(1, E) if step == 0 else pl.ds(E if step > 0 else 1, 1)


def landing_span(step):
    return pl.ds(1, E) if step == 0 else pl.ds(0 if step > 0 else E + 1, 1)


def column(row):
    spread = jnp.broadcast_to(row, (C, C))
    on_diagonal = lax.broadcasted_iota(jnp.int32, (C, C), 0) == lax.broadcasted_iota(jnp.int32, (C, C), 1)
    return jnp.sum(jnp.where(on_diagonal, spread, 0.0), axis=1, keepdims=True)


def prepare_weight(held, ready):
    for c in range(3):
        rows = pl.ds(c * C, C)
        for pair in range(TAPS // 2):
            both = jnp.concatenate([held[(2 * pair) * 3 + c], held[(2 * pair + 1) * 3 + c]], axis=1)
            ready[rows, pl.ds(pair * 2 * C, 2 * C)] = both
        ready[rows, pl.ds((TAPS - 1) * C, C)] = held[(TAPS - 1) * 3 + c]


def conv_pair(src, ready, bias, mask, spots, put):
    stacked = []
    for a in range(3):
        for b in range(3):
            stacked.append(jnp.concatenate([src[x + a - 1, y + b - 1] for x, y in spots], axis=1))
    sums = jnp.dot(ready[...], jnp.concatenate(stacked, axis=0), preferred_element_type=jnp.float32)
    lane = lax.broadcasted_iota(jnp.int32, (C, Z), 1)
    for half, (x, y) in enumerate(spots):
        part = sums[:, half * Z : (half + 1) * Z]
        before = jnp.where(lane == 0, 0.0, pltpu.roll(part[:C], 1, 1))
        after = jnp.where(lane == Z - 1, 0.0, pltpu.roll(part[2 * C :], Z - 1, 1))
        value = part[C : 2 * C] + before + after + bias
        put(x, y, (jnp.maximum(value, 0.0) * mask).astype(jnp.bfloat16))


def interior(step, pair):
    def body(i, carry):
        for y in range(2, E, 2):
            pair(((i, y), (i, y + 1)))
        return carry

    lax.fori_loop(2, E, body, 0)


def x_rows(pair):
    def body(i, carry):
        x = 1 + i * (E - 1)
        for y in range(2, E, 2):
            pair(((x, y), (x, y + 1)))
        return carry

    lax.fori_loop(0, 2, body, 0)


def y_columns(pair):
    def body(i, carry):
        x = 1 + 2 * i
        for y in (1, E):
            pair(((x, y), (x + 1, y)))
        return carry

    lax.fori_loop(0, E // 2, body, 0)


def remote_kernel(
    shape, feat_hbm, occ_ref, w1_hbm, b1_ref, w2_hbm, b2_ref, second_ref,
    feat, stage, first_in, second_in, w_held, w1, w2, mask_ref, bias_ref, copy_sem, send_sem, recv_sem,
):
    n_region, n_dev = shape
    region, dev = lax.axis_index("region"), lax.axis_index("dev")
    loads = [
        pltpu.make_async_copy(feat_hbm, feat, copy_sem.at[0]),
        pltpu.make_async_copy(w1_hbm, w_held.at[0], copy_sem.at[1]),
        pltpu.make_async_copy(w2_hbm, w_held.at[1], copy_sem.at[2]),
    ]
    for load in loads:
        load.start()

    def there(dr, dd):
        r, d = region + dr, dev + dd
        return (r >= 0) & (r < n_region) & (d >= 0) & (d < n_dev)

    barrier = pltpu.get_barrier_semaphore()
    count = 0
    for dr, dd in WAYS:
        here = there(dr, dd)
        count = count + here.astype(jnp.int32)

        @pl.when(here)
        def _():
            pl.semaphore_signal(barrier, inc=1, device_id=(region + dr, dev + dd), device_id_type=MESH)

    def transfers(buf, turn):
        made = []
        for k, (dr, dd) in enumerate(WAYS):
            copy = pltpu.make_async_remote_copy(
                src_ref=buf.at[source_span(dr), source_span(dd)],
                dst_ref=buf.at[landing_span(dr), landing_span(dd)],
                send_sem=send_sem.at[turn, k],
                recv_sem=recv_sem.at[turn, k],
                device_id=(region + dr, dev + dd),
                device_id_type=MESH,
            )
            made.append((copy, there(dr, dd), there(-dr, -dd)))
        return made

    def start(made):
        for copy, goes, _ in made:
            pl.when(goes)(copy.start)

    def arrived(made):
        for copy, _, comes in made:
            pl.when(comes)(copy.wait_recv)

    def sent(made):
        for copy, goes, _ in made:
            pl.when(goes)(copy.wait_send)

    for dr, dd in WAYS:

        @pl.when(jnp.logical_not(there(-dr, -dd)))
        def _():
            nx, ny = (E if dr == 0 else 1), (E if dd == 0 else 1)
            for buf in (first_in, second_in):
                buf[landing_span(dr), landing_span(dd)] = jnp.zeros((nx, ny, C, Z), jnp.bfloat16)

    mine = occ_ref[region].astype(jnp.float32)
    bricks, devs = mine.shape
    picked = jnp.where(lax.broadcasted_iota(jnp.int32, (bricks, devs), 1) == dev, mine, 0.0)
    level = jnp.sum(picked, axis=1, keepdims=True)
    brick = lax.broadcasted_iota(jnp.int32, (bricks, Z), 0)
    voxel = lax.broadcasted_iota(jnp.int32, (bricks, Z), 1)
    span = Z // bricks
    inside = (voxel >= brick * span) & (voxel < (brick + 1) * span)
    mask_ref[...] = jnp.sum(jnp.where(inside, level, 0.0), axis=0, keepdims=True)
    bias_ref[0] = jnp.broadcast_to(column(b1_ref[...]), (C, Z))
    bias_ref[1] = jnp.broadcast_to(column(b2_ref[...]), (C, Z))
    mask = mask_ref[...]

    loads[0].wait()
    rows = feat.shape[0]
    chunk = 256

    def widen(i, carry):
        at = pl.ds(pl.multiple_of(i * chunk, chunk), chunk)
        stage[at, :] = jnp.where(mask > 0, feat[at, :].astype(jnp.float32), 0.0)
        return carry

    lax.fori_loop(0, rows // chunk, widen, 0)

    def regroup(x, carry):
        for y in range(E):
            first_in[x + 1, y + 1] = stage[pl.ds(x * E + y, C, stride=E * E), :].astype(jnp.bfloat16)
        return carry

    lax.fori_loop(0, E, regroup, 0)

    pl.semaphore_wait(barrier, count)
    one = transfers(first_in, 0)
    start(one)
    loads[1].wait()
    prepare_weight(w_held.at[0], w1)
    loads[2].wait()
    prepare_weight(w_held.at[1], w2)

    def put_first(x, y, value):
        second_in[x, y] = value

    def put_second(x, y, value):
        second_ref[x - 1, y - 1] = value

    def pair_one(spots):
        conv_pair(first_in, w1, bias_ref[0], mask, spots, put_first)

    def pair_two(spots):
        conv_pair(second_in, w2, bias_ref[1], mask, spots, put_second)

    interior(0, pair_one)
    arrived(one[2:4])
    x_rows(pair_one)
    arrived(one[:2])
    arrived(one[4:])
    y_columns(pair_one)
    two = transfers(second_in, 1)
    start(two)
    interior(1, pair_two)
    arrived(two[2:4])
    x_rows(pair_two)
    arrived(two[:2])
    arrived(two[4:])
    y_columns(pair_two)
    sent(one)
    sent(two)


def local_kernel(second_ref, wd_ref, bd_ref, skip_ref, down_ref, stage, wide, wd, narrow):
    def spread(x, carry):
        for y in range(E):
            stage[pl.ds(x * E + y, C, stride=E * E), :] = second_ref[x, y].astype(jnp.float32)
        return carry

    lax.fori_loop(0, E, spread, 0)
    rows = stage.shape[0]
    chunk = 256

    def pack(i, carry):
        at = pl.ds(pl.multiple_of(i * chunk, chunk), chunk)
        skip_ref[at, :] = stage[at, :].astype(jnp.bfloat16)
        return carry

    lax.fori_loop(0, rows // chunk, pack, 0)

    wide[...] = wd_ref[...].astype(jnp.float32)
    for c in range(2):
        for a in range(2):
            both = [wide[pl.ds(a * 4 + b * 2 + c, C, stride=8), :].astype(jnp.bfloat16) for b in range(2)]
            wd[pl.ds(c * C, C), pl.ds(a * 2 * C, 2 * C)] = jnp.concatenate(both, axis=1)
    lane_in = lax.broadcasted_iota(jnp.int32, (2 * Z, Z), 0)
    lane_out = lax.broadcasted_iota(jnp.int32, (2 * Z, Z), 1)
    keep = jnp.where(lane_in == 2 * lane_out, 1.0, 0.0).astype(jnp.bfloat16)
    bias = jnp.broadcast_to(column(bd_ref[...]), (C, 2 * Z))
    half = E // 2

    def lower(x, carry):
        for y in range(0, E, 4):
            stacked = [
                jnp.concatenate([second_ref[2 * x + a, y + 2 * k + b] for k in range(2)], axis=1)
                for a in range(2)
                for b in range(2)
            ]
            sums = jnp.dot(wd[...], jnp.concatenate(stacked, axis=0), preferred_element_type=jnp.float32)
            moved = jnp.concatenate([pltpu.roll(sums[C:, k * Z : (k + 1) * Z], Z - 1, 1) for k in range(2)], axis=1)
            value = jnp.maximum(sums[:C] + moved + bias, 0.0).astype(jnp.bfloat16)
            narrow[y // 4, pl.ds(x, C, stride=half), :] = jnp.dot(value, keep, preferred_element_type=jnp.float32)
        return carry

    lax.fori_loop(0, half, lower, 0)
    for k in range(2):
        down_ref[:, :, pl.ds(k * Z, Z)] = narrow[k].reshape(C, half, Z).astype(jnp.bfloat16)


def on_device(shape, features, occupancy, weight_one, bias_one, weight_two, bias_two, weight_down, bias_down):
    bf16, f32 = jnp.bfloat16, jnp.float32
    any_space = pl.BlockSpec(memory_space=pl.ANY)
    vmem = pl.BlockSpec(memory_space=pltpu.VMEM)
    rows = C * E * E
    held = [w.transpose(2, 3, 4, 0, 1).reshape(27, C, C) for w in (weight_one, weight_two)]
    second = pl.pallas_call(
        functools.partial(remote_kernel, shape),
        out_shape=jax.ShapeDtypeStruct((E, E, C, Z), bf16),
        in_specs=[any_space, vmem, any_space, vmem, any_space, vmem],
        out_specs=vmem,
        scratch_shapes=[
            pltpu.VMEM((rows, Z), bf16),
            pltpu.VMEM((rows, Z), f32),
            pltpu.VMEM((E + 2, E + 2, C, Z), bf16),
            pltpu.VMEM((E + 2, E + 2, C, Z), bf16),
            pltpu.VMEM((2, 27, C, C), bf16),
            pltpu.VMEM((3 * C, TAPS * C), bf16),
            pltpu.VMEM((3 * C, TAPS * C), bf16),
            pltpu.VMEM((1, Z), f32),
            pltpu.VMEM((2, C, Z), f32),
            pltpu.SemaphoreType.DMA((3,)),
            pltpu.SemaphoreType.DMA((2, len(WAYS))),
            pltpu.SemaphoreType.DMA((2, len(WAYS))),
        ],
        compiler_params=pltpu.CompilerParams(
            collective_id=0, has_side_effects=True, vmem_limit_bytes=32 * 1024 * 1024
        ),
        name="halo_convs",
    )(
        features.reshape(rows, Z),
        occupancy.transpose(0, 2, 1),
        held[0],
        bias_one.reshape(1, C),
        held[1],
        bias_two.reshape(1, C),
    )
    skip, down = pl.pallas_call(
        local_kernel,
        out_shape=(
            jax.ShapeDtypeStruct((rows, Z), bf16),
            jax.ShapeDtypeStruct((C, E // 2, 2 * Z), bf16),
        ),
        in_specs=[vmem] * 3,
        out_specs=(vmem, vmem),
        scratch_shapes=[
            pltpu.VMEM((rows, Z), f32),
            pltpu.VMEM((8 * C, C), f32),
            pltpu.VMEM((2 * C, 4 * C), bf16),
            pltpu.VMEM((2, C * E // 2, Z), f32),
        ],
        compiler_params=pltpu.CompilerParams(vmem_limit_bytes=32 * 1024 * 1024),
        name="skip_and_down",
    )(second, weight_down.transpose(0, 2, 3, 4, 1).reshape(8 * C, C), bias_down.reshape(1, C))
    return skip.reshape(C, E, E, Z), down


def solution(mesh):
    return jax.shard_map(
        functools.partial(on_device, (mesh.shape["region"], mesh.shape["dev"])),
        mesh=mesh,
        in_specs=(P(None, "region", "dev", None), P(), P(), P(), P(), P(), P(), P()),
        out_specs=(P(None, "region", "dev", None), P(None, "region", "dev")),
        check_vma=False,
    )
```

```python
import functools

import jax
import jax.numpy as jnp
from jax import lax
from jax.experimental import pallas as pl
from jax.experimental.pallas import tpu as pltpu
from jax.sharding import PartitionSpec as P

MESH = pl.DeviceIdType.MESH
WAYS = ((0, 1), (0, -1), (1, 0), (-1, 0), (1, 1), (1, -1), (-1, 1), (-1, -1))
E = 8
C = 64
Z = 128
TAPS = 9


def source_span(step):
    return pl.ds(1, E) if step == 0 else pl.ds(E if step > 0 else 1, 1)


def landing_span(step):
    return pl.ds(1, E) if step == 0 else pl.ds(0 if step > 0 else E + 1, 1)


def column(row):
    spread = jnp.broadcast_to(row, (C, C))
    on_diagonal = lax.broadcasted_iota(jnp.int32, (C, C), 0) == lax.broadcasted_iota(jnp.int32, (C, C), 1)
    return jnp.sum(jnp.where(on_diagonal, spread, 0.0), axis=1, keepdims=True)


def prepare_weight(held, ready):
    for c in range(3):
        rows = pl.ds(c * C, C)
        for pair in range(TAPS // 2):
            both = jnp.concatenate([held[(2 * pair) * 3 + c], held[(2 * pair + 1) * 3 + c]], axis=1)
            ready[rows, pl.ds(pair * 2 * C, 2 * C)] = both
        ready[rows, pl.ds((TAPS - 1) * C, C)] = held[(TAPS - 1) * 3 + c]


def conv_pair(src, ready, bias, mask, spots, put):
    stacked = []
    for a in range(3):
        for b in range(3):
            stacked.append(jnp.concatenate([src[x + a - 1, y + b - 1] for x, y in spots], axis=1))
    sums = jnp.dot(ready[...], jnp.concatenate(stacked, axis=0), preferred_element_type=jnp.float32)
    lane = lax.broadcasted_iota(jnp.int32, (C, Z), 1)
    for half, (x, y) in enumerate(spots):
        part = sums[:, half * Z : (half + 1) * Z]
        before = jnp.where(lane == 0, 0.0, pltpu.roll(part[:C], 1, 1))
        after = jnp.where(lane == Z - 1, 0.0, pltpu.roll(part[2 * C :], Z - 1, 1))
        value = part[C : 2 * C] + before + after + bias
        put(x, y, (jnp.maximum(value, 0.0) * mask).astype(jnp.bfloat16))


def interior(pair):
    for x in range(2, E):
        for y in range(2, E, 2):
            pair(((x, y), (x, y + 1)))


def x_rows(pair):
    for x in (1, E):
        for y in range(2, E, 2):
            pair(((x, y), (x, y + 1)))


def y_columns(pair):
    for x in range(1, E, 2):
        for y in (1, E):
            pair(((x, y), (x + 1, y)))


def remote_kernel(
    shape, feat_hbm, occ_hbm, w1_hbm, b1_hbm, w2_hbm, b2_hbm, second_ref,
    feat, occ_ref, b_held, first_in, second_in, w_held, w1, w2, mask_ref, bias_ref, copy_sem, send_sem, recv_sem,
):
    n_region, n_dev = shape
    region, dev = lax.axis_index("region"), lax.axis_index("dev")
    loads = [
        pltpu.make_async_copy(feat_hbm, feat, copy_sem.at[0]),
        pltpu.make_async_copy(w1_hbm, w_held.at[0], copy_sem.at[1]),
        pltpu.make_async_copy(w2_hbm, w_held.at[1], copy_sem.at[2]),
        pltpu.make_async_copy(occ_hbm, occ_ref, copy_sem.at[3]),
        pltpu.make_async_copy(b1_hbm, b_held.at[0], copy_sem.at[4]),
        pltpu.make_async_copy(b2_hbm, b_held.at[1], copy_sem.at[5]),
    ]
    for load in loads:
        load.start()

    def there(dr, dd):
        r, d = region + dr, dev + dd
        return (r >= 0) & (r < n_region) & (d >= 0) & (d < n_dev)

    barrier = pltpu.get_barrier_semaphore()
    count = 0
    for dr, dd in WAYS:
        here = there(dr, dd)
        count = count + here.astype(jnp.int32)

        @pl.when(here)
        def _():
            pl.semaphore_signal(barrier, inc=1, device_id=(region + dr, dev + dd), device_id_type=MESH)

    def transfers(buf, turn):
        made = []
        for k, (dr, dd) in enumerate(WAYS):
            copy = pltpu.make_async_remote_copy(
                src_ref=buf.at[source_span(dr), source_span(dd)],
                dst_ref=buf.at[landing_span(dr), landing_span(dd)],
                send_sem=send_sem.at[turn, k],
                recv_sem=recv_sem.at[turn, k],
                device_id=(region + dr, dev + dd),
                device_id_type=MESH,
            )
            made.append((copy, there(dr, dd), there(-dr, -dd)))
        return made

    def start(made):
        for copy, goes, _ in made:
            pl.when(goes)(copy.start)

    def arrived(made):
        for copy, _, comes in made:
            pl.when(comes)(copy.wait_recv)

    def sent(made):
        for copy, goes, _ in made:
            pl.when(goes)(copy.wait_send)

    for dr, dd in WAYS:

        @pl.when(jnp.logical_not(there(-dr, -dd)))
        def _():
            nx, ny = (E if dr == 0 else 1), (E if dd == 0 else 1)
            for buf in (first_in, second_in):
                buf[landing_span(dr), landing_span(dd)] = jnp.zeros((nx, ny, C, Z), jnp.bfloat16)

    loads[3].wait()
    mine = occ_ref[region].astype(jnp.float32)
    bricks, devs = mine.shape
    picked = jnp.where(lax.broadcasted_iota(jnp.int32, (bricks, devs), 1) == dev, mine, 0.0)
    level = jnp.sum(picked, axis=1, keepdims=True)
    brick = lax.broadcasted_iota(jnp.int32, (bricks, Z), 0)
    voxel = lax.broadcasted_iota(jnp.int32, (bricks, Z), 1)
    span = Z // bricks
    inside = (voxel >= brick * span) & (voxel < (brick + 1) * span)
    mask_ref[...] = jnp.sum(jnp.where(inside, level, 0.0), axis=0, keepdims=True)
    mask = mask_ref[...]

    loads[0].wait()
    for x in range(0, E, 2):
        slab = jnp.concatenate([feat[pl.ds(c * E * E + x * E, 2 * E), :] for c in range(C)], axis=0)
        blocks = jnp.swapaxes(slab.reshape(C, 2 * E, Z), 0, 1)
        blocks = jnp.where(mask[None] > 0, blocks, jnp.zeros_like(blocks))
        for k in range(2):
            first_in[x + k + 1, pl.ds(1, E)] = blocks[k * E : (k + 1) * E]

    pl.semaphore_wait(barrier, count)
    one = transfers(first_in, 0)
    start(one)
    loads[1].wait()
    prepare_weight(w_held.at[0], w1)
    loads[2].wait()
    prepare_weight(w_held.at[1], w2)
    for k in range(2):
        loads[4 + k].wait()
        bias_ref[k] = jnp.broadcast_to(column(b_held[k]), (C, Z))

    def put_first(x, y, value):
        second_in[x, y] = value

    def put_second(x, y, value):
        second_ref[x - 1, y - 1] = value

    def pair_one(spots):
        conv_pair(first_in, w1, bias_ref[0], mask, spots, put_first)

    def pair_two(spots):
        conv_pair(second_in, w2, bias_ref[1], mask, spots, put_second)

    interior(pair_one)
    arrived(one[2:4])
    x_rows(pair_one)
    arrived(one[:2])
    arrived(one[4:])
    y_columns(pair_one)
    two = transfers(second_in, 1)
    start(two)
    interior(pair_two)
    arrived(two[2:4])
    x_rows(pair_two)
    arrived(two[:2])
    arrived(two[4:])
    y_columns(pair_two)
    sent(one)
    sent(two)


def local_kernel(second_ref, wd_ref, bd_ref, skip_ref, down_ref, wide, wd, narrow):
    for x in range(0, E, 2):
        blocks = jnp.swapaxes(jnp.concatenate([second_ref[x], second_ref[x + 1]], axis=0), 0, 1)
        for o in range(C):
            skip_ref[pl.ds(o * E * E + x * E, 2 * E), :] = blocks[o]

    wide[...] = wd_ref[...].astype(jnp.float32)
    for c in range(2):
        for a in range(2):
            both = [wide[pl.ds(a * 4 + b * 2 + c, C, stride=8), :].astype(jnp.bfloat16) for b in range(2)]
            wd[pl.ds(c * C, C), pl.ds(a * 2 * C, 2 * C)] = jnp.concatenate(both, axis=1)
    lane_in = lax.broadcasted_iota(jnp.int32, (2 * Z, Z), 0)
    lane_out = lax.broadcasted_iota(jnp.int32, (2 * Z, Z), 1)
    keep = jnp.where(lane_in == 2 * lane_out, 1.0, 0.0).astype(jnp.bfloat16)
    bias = jnp.broadcast_to(column(bd_ref[...]), (C, 2 * Z))
    half = E // 2

    for x in range(half):
        for y in range(0, E, 4):
            stacked = [
                jnp.concatenate([second_ref[2 * x + a, y + 2 * k + b] for k in range(2)], axis=1)
                for a in range(2)
                for b in range(2)
            ]
            sums = jnp.dot(wd[...], jnp.concatenate(stacked, axis=0), preferred_element_type=jnp.float32)
            moved = jnp.concatenate([pltpu.roll(sums[C:, k * Z : (k + 1) * Z], Z - 1, 1) for k in range(2)], axis=1)
            value = jnp.maximum(sums[:C] + moved + bias, 0.0).astype(jnp.bfloat16)
            narrow[y // 4, pl.ds(x, C, stride=half), :] = jnp.dot(value, keep, preferred_element_type=jnp.float32)
    for k in range(2):
        down_ref[:, :, pl.ds(k * Z, Z)] = narrow[k].reshape(C, half, Z).astype(jnp.bfloat16)


def on_device(shape, features, occupancy, weight_one, bias_one, weight_two, bias_two, weight_down, bias_down):
    bf16, f32 = jnp.bfloat16, jnp.float32
    hbm = pl.BlockSpec(memory_space=pltpu.HBM)
    vmem = pl.BlockSpec(memory_space=pltpu.VMEM)
    rows = C * E * E
    held = [w.transpose(2, 3, 4, 0, 1).reshape(27, C, C) for w in (weight_one, weight_two)]
    second = pl.pallas_call(
        functools.partial(remote_kernel, shape),
        out_shape=jax.ShapeDtypeStruct((E, E, C, Z), bf16),
        in_specs=[hbm] * 6,
        out_specs=vmem,
        scratch_shapes=[
            pltpu.VMEM((rows, Z), bf16),
            pltpu.VMEM((shape[0], occupancy.shape[2], shape[1]), jnp.int32),
            pltpu.VMEM((2, 1, C), f32),
            pltpu.VMEM((E + 2, E + 2, C, Z), bf16),
            pltpu.VMEM((E + 2, E + 2, C, Z), bf16),
            pltpu.VMEM((2, 27, C, C), bf16),
            pltpu.VMEM((3 * C, TAPS * C), bf16),
            pltpu.VMEM((3 * C, TAPS * C), bf16),
            pltpu.VMEM((1, Z), f32),
            pltpu.VMEM((2, C, Z), f32),
            pltpu.SemaphoreType.DMA((6,)),
            pltpu.SemaphoreType.DMA((2, len(WAYS))),
            pltpu.SemaphoreType.DMA((2, len(WAYS))),
        ],
        compiler_params=pltpu.CompilerParams(
            collective_id=0, has_side_effects=True, vmem_limit_bytes=32 * 1024 * 1024
        ),
        name="halo_convs",
    )(
        features.reshape(rows, Z),
        occupancy.transpose(0, 2, 1),
        held[0],
        bias_one.reshape(1, C),
        held[1],
        bias_two.reshape(1, C),
    )
    skip, down = pl.pallas_call(
        local_kernel,
        out_shape=(
            jax.ShapeDtypeStruct((rows, Z), bf16),
            jax.ShapeDtypeStruct((C, E // 2, 2 * Z), bf16),
        ),
        in_specs=[vmem] * 3,
        out_specs=(vmem, vmem),
        scratch_shapes=[
            pltpu.VMEM((8 * C, C), f32),
            pltpu.VMEM((2 * C, 4 * C), bf16),
            pltpu.VMEM((2, C * E // 2, Z), f32),
        ],
        compiler_params=pltpu.CompilerParams(vmem_limit_bytes=32 * 1024 * 1024),
        name="skip_and_down",
    )(second, weight_down.transpose(0, 2, 3, 4, 1).reshape(8 * C, C), bias_down.reshape(1, C))
    return skip.reshape(C, E, E, Z), down


def solution(mesh):
    return jax.shard_map(
        functools.partial(on_device, (mesh.shape["region"], mesh.shape["dev"])),
        mesh=mesh,
        in_specs=(P(None, "region", "dev", None), P(), P(), P(), P(), P(), P(), P()),
        out_specs=(P(None, "region", "dev", None), P(None, "region", "dev")),
        check_vma=False,
    )
```

```python
import functools

import jax
import jax.numpy as jnp
from jax import lax
from jax.experimental import pallas as pl
from jax.experimental.pallas import tpu as pltpu
from jax.sharding import PartitionSpec as P

MESH = pl.DeviceIdType.MESH
WAYS = ((0, 1), (0, -1), (1, 0), (-1, 0), (1, 1), (1, -1), (-1, 1), (-1, -1))
E = 8
C = 64
Z = 128
TAPS = 9


def source_span(step):
    return pl.ds(1, E) if step == 0 else pl.ds(E if step > 0 else 1, 1)


def landing_span(step):
    return pl.ds(1, E) if step == 0 else pl.ds(0 if step > 0 else E + 1, 1)


def column(row):
    spread = jnp.broadcast_to(row, (C, C))
    on_diagonal = lax.broadcasted_iota(jnp.int32, (C, C), 0) == lax.broadcasted_iota(jnp.int32, (C, C), 1)
    return jnp.sum(jnp.where(on_diagonal, spread, 0.0), axis=1, keepdims=True)


def prepare_weight(held, ready):
    for c in range(3):
        rows = pl.ds(c * C, C)
        for pair in range(TAPS // 2):
            both = jnp.concatenate([held[(2 * pair) * 3 + c], held[(2 * pair + 1) * 3 + c]], axis=1)
            ready[rows, pl.ds(pair * 2 * C, 2 * C)] = both
        ready[rows, pl.ds((TAPS - 1) * C, C)] = held[(TAPS - 1) * 3 + c]


def conv_pair(src, ready, bias, mask, spots, put):
    stacked = []
    for a in range(3):
        for b in range(3):
            stacked.append(jnp.concatenate([src[x + a - 1, y + b - 1] for x, y in spots], axis=1))
    sums = jnp.dot(ready[...], jnp.concatenate(stacked, axis=0), preferred_element_type=jnp.float32)
    lane = lax.broadcasted_iota(jnp.int32, (C, Z), 1)
    for half, (x, y) in enumerate(spots):
        part = sums[:, half * Z : (half + 1) * Z]
        before = jnp.where(lane == 0, 0.0, pltpu.roll(part[:C], 1, 1))
        after = jnp.where(lane == Z - 1, 0.0, pltpu.roll(part[2 * C :], Z - 1, 1))
        value = part[C : 2 * C] + before + after + bias
        put(x, y, (jnp.maximum(value, 0.0) * mask).astype(jnp.bfloat16))


def interior(pair):
    for x in range(2, E):
        for y in range(2, E, 2):
            pair(((x, y), (x, y + 1)))


def x_rows(pair):
    for x in (1, E):
        for y in range(2, E, 2):
            pair(((x, y), (x, y + 1)))


def y_columns(pair):
    for x in range(1, E, 2):
        for y in (1, E):
            pair(((x, y), (x + 1, y)))


def remote_kernel(
    shape, feat_hbm, occ_hbm, w1_hbm, b1_hbm, w2_hbm, b2_hbm, second_ref,
    feat, occ_ref, b_held, first_in, second_in, w_held, w1, w2, mask_ref, bias_ref, copy_sem, send_sem, recv_sem,
):
    n_region, n_dev = shape
    region, dev = lax.axis_index("region"), lax.axis_index("dev")
    loads = [
        pltpu.make_async_copy(feat_hbm, feat, copy_sem.at[0]),
        pltpu.make_async_copy(w1_hbm, w_held.at[0], copy_sem.at[1]),
        pltpu.make_async_copy(w2_hbm, w_held.at[1], copy_sem.at[2]),
        pltpu.make_async_copy(occ_hbm, occ_ref, copy_sem.at[3]),
        pltpu.make_async_copy(b1_hbm, b_held.at[0], copy_sem.at[4]),
        pltpu.make_async_copy(b2_hbm, b_held.at[1], copy_sem.at[5]),
    ]
    for load in loads:
        load.start()

    def there(dr, dd):
        r, d = region + dr, dev + dd
        return (r >= 0) & (r < n_region) & (d >= 0) & (d < n_dev)

    barrier = pltpu.get_barrier_semaphore()
    count = 0
    for dr, dd in WAYS:
        here = there(dr, dd)
        count = count + here.astype(jnp.int32)

        @pl.when(here)
        def _():
            pl.semaphore_signal(barrier, inc=1, device_id=(region + dr, dev + dd), device_id_type=MESH)

    def transfers(buf, turn):
        made = []
        for k, (dr, dd) in enumerate(WAYS):
            copy = pltpu.make_async_remote_copy(
                src_ref=buf.at[source_span(dr), source_span(dd)],
                dst_ref=buf.at[landing_span(dr), landing_span(dd)],
                send_sem=send_sem.at[turn, k],
                recv_sem=recv_sem.at[turn, k],
                device_id=(region + dr, dev + dd),
                device_id_type=MESH,
            )
            made.append((copy, there(dr, dd), there(-dr, -dd)))
        return made

    def start(made):
        for copy, goes, _ in made:
            pl.when(goes)(copy.start)

    def arrived(made):
        for copy, _, comes in made:
            pl.when(comes)(copy.wait_recv)

    def sent(made):
        for copy, goes, _ in made:
            pl.when(goes)(copy.wait_send)

    for dr, dd in WAYS:

        @pl.when(jnp.logical_not(there(-dr, -dd)))
        def _():
            nx, ny = (E if dr == 0 else 1), (E if dd == 0 else 1)
            for buf in (first_in, second_in):
                buf[landing_span(dr), landing_span(dd)] = jnp.zeros((nx, ny, C, Z), jnp.bfloat16)

    loads[3].wait()
    mine = occ_ref[region].astype(jnp.float32)
    bricks, devs = mine.shape
    picked = jnp.where(lax.broadcasted_iota(jnp.int32, (bricks, devs), 1) == dev, mine, 0.0)
    level = jnp.sum(picked, axis=1, keepdims=True)
    brick = lax.broadcasted_iota(jnp.int32, (bricks, Z), 0)
    voxel = lax.broadcasted_iota(jnp.int32, (bricks, Z), 1)
    span = Z // bricks
    inside = (voxel >= brick * span) & (voxel < (brick + 1) * span)
    mask_ref[...] = jnp.sum(jnp.where(inside, level, 0.0), axis=0, keepdims=True)
    mask = mask_ref[...]

    loads[0].wait()
    for x in range(0, E, 2):
        slab = jnp.concatenate([feat[pl.ds(c * E * E + x * E, 2 * E), :] for c in range(C)], axis=0)
        blocks = jnp.swapaxes(slab.reshape(C, 2 * E, Z), 0, 1)
        blocks = jnp.where(mask[None] > 0, blocks, jnp.zeros_like(blocks))
        for k in range(2):
            first_in[x + k + 1, pl.ds(1, E)] = blocks[k * E : (k + 1) * E]

    pl.semaphore_wait(barrier, count)
    one = transfers(first_in, 0)
    start(one)
    loads[1].wait()
    prepare_weight(w_held.at[0], w1)
    loads[2].wait()
    prepare_weight(w_held.at[1], w2)
    for k in range(2):
        loads[4 + k].wait()
        bias_ref[k] = jnp.broadcast_to(column(b_held[k]), (C, Z))

    def put_first(x, y, value):
        second_in[x, y] = value

    def put_second(x, y, value):
        second_ref[x - 1, y - 1] = value

    def pair_one(spots):
        conv_pair(first_in, w1, bias_ref[0], mask, spots, put_first)

    def pair_two(spots):
        conv_pair(second_in, w2, bias_ref[1], mask, spots, put_second)

    interior(pair_one)
    arrived(one[2:4])
    x_rows(pair_one)
    arrived(one[:2])
    arrived(one[4:])
    y_columns(pair_one)
    two = transfers(second_in, 1)
    start(two)
    interior(pair_two)
    arrived(two[2:4])
    x_rows(pair_two)
    arrived(two[:2])
    arrived(two[4:])
    y_columns(pair_two)
    sent(one)
    sent(two)


def local_kernel(second_ref, wd_ref, bd_ref, skip_ref, down_ref, wide, wd, narrow):
    for x in range(0, E, 2):
        blocks = jnp.swapaxes(jnp.concatenate([second_ref[x], second_ref[x + 1]], axis=0), 0, 1)
        for o in range(C):
            skip_ref[pl.ds(o * E * E + x * E, 2 * E), :] = blocks[o]

    wide[...] = wd_ref[...].astype(jnp.float32)
    for c in range(2):
        for a in range(2):
            both = [wide[pl.ds(a * 4 + b * 2 + c, C, stride=8), :].astype(jnp.bfloat16) for b in range(2)]
            wd[pl.ds(c * C, C), pl.ds(a * 2 * C, 2 * C)] = jnp.concatenate(both, axis=1)
    lane_in = lax.broadcasted_iota(jnp.int32, (2 * Z, Z), 0)
    lane_out = lax.broadcasted_iota(jnp.int32, (2 * Z, Z), 1)
    keep = jnp.where(lane_in == 2 * lane_out, 1.0, 0.0).astype(jnp.bfloat16)
    bias = jnp.broadcast_to(column(bd_ref[...]), (C, 2 * Z))
    half = E // 2

    for x in range(half):
        for y in range(0, E, 4):
            stacked = [
                jnp.concatenate([second_ref[2 * x + a, y + 2 * k + b] for k in range(2)], axis=1)
                for a in range(2)
                for b in range(2)
            ]
            sums = jnp.dot(wd[...], jnp.concatenate(stacked, axis=0), preferred_element_type=jnp.float32)
            moved = jnp.concatenate([pltpu.roll(sums[C:, k * Z : (k + 1) * Z], Z - 1, 1) for k in range(2)], axis=1)
            value = jnp.maximum(sums[:C] + moved + bias, 0.0).astype(jnp.bfloat16)
            narrow[y // 4, pl.ds(x, C, stride=half), :] = jnp.dot(value, keep, preferred_element_type=jnp.float32)
    for k in range(2):
        down_ref[:, :, pl.ds(k * Z, Z)] = narrow[k].reshape(C, half, Z).astype(jnp.bfloat16)


def on_device(shape, features, occupancy, weight_one, bias_one, weight_two, bias_two, weight_down, bias_down):
    bf16, f32 = jnp.bfloat16, jnp.float32
    hbm = pl.BlockSpec(memory_space=pltpu.HBM)
    vmem = pl.BlockSpec(memory_space=pltpu.VMEM)
    rows = C * E * E
    held = [w.transpose(2, 3, 4, 0, 1).reshape(27, C, C) for w in (weight_one, weight_two)]
    second = pl.pallas_call(
        functools.partial(remote_kernel, shape),
        out_shape=jax.ShapeDtypeStruct((E, E, C, Z), bf16),
        in_specs=[hbm] * 6,
        out_specs=vmem,
        scratch_shapes=[
            pltpu.VMEM((rows, Z), bf16),
            pltpu.VMEM((shape[0], occupancy.shape[2], shape[1]), jnp.int32),
            pltpu.VMEM((2, 1, C), f32),
            pltpu.VMEM((E + 2, E + 2, C, Z), bf16),
            pltpu.VMEM((E + 2, E + 2, C, Z), bf16),
            pltpu.VMEM((2, 27, C, C), bf16),
            pltpu.VMEM((3 * C, TAPS * C), bf16),
            pltpu.VMEM((3 * C, TAPS * C), bf16),
            pltpu.VMEM((1, Z), f32),
            pltpu.VMEM((2, C, Z), f32),
            pltpu.SemaphoreType.DMA((6,)),
            pltpu.SemaphoreType.DMA((2, len(WAYS))),
            pltpu.SemaphoreType.DMA((2, len(WAYS))),
        ],
        compiler_params=pltpu.CompilerParams(
            collective_id=0, has_side_effects=True, vmem_limit_bytes=32 * 1024 * 1024
        ),
        name="halo_convs",
    )(
        *(
            pltpu.with_memory_space_constraint(operand, pltpu.HBM)
            for operand in (
                features.reshape(rows, Z),
                occupancy.transpose(0, 2, 1),
                held[0],
                bias_one.reshape(1, C),
                held[1],
                bias_two.reshape(1, C),
            )
        )
    )
    skip, down = pl.pallas_call(
        local_kernel,
        out_shape=(
            jax.ShapeDtypeStruct((rows, Z), bf16),
            jax.ShapeDtypeStruct((C, E // 2, 2 * Z), bf16),
        ),
        in_specs=[vmem] * 3,
        out_specs=(vmem, vmem),
        scratch_shapes=[
            pltpu.VMEM((8 * C, C), f32),
            pltpu.VMEM((2 * C, 4 * C), bf16),
            pltpu.VMEM((2, C * E // 2, Z), f32),
        ],
        compiler_params=pltpu.CompilerParams(vmem_limit_bytes=32 * 1024 * 1024),
        name="skip_and_down",
    )(second, weight_down.transpose(0, 2, 3, 4, 1).reshape(8 * C, C), bias_down.reshape(1, C))
    return skip.reshape(C, E, E, Z), down


def solution(mesh):
    return jax.shard_map(
        functools.partial(on_device, (mesh.shape["region"], mesh.shape["dev"])),
        mesh=mesh,
        in_specs=(P(None, "region", "dev", None), P(), P(), P(), P(), P(), P(), P()),
        out_specs=(P(None, "region", "dev", None), P(None, "region", "dev")),
        check_vma=False,
    )
```

```python
import functools

import jax
import jax.numpy as jnp
from jax import lax
from jax.experimental import pallas as pl
from jax.experimental.pallas import tpu as pltpu
from jax.sharding import PartitionSpec as P

MESH = pl.DeviceIdType.MESH
CORNERS = ((1, 1), (-1, 1), (1, -1), (-1, -1))
FACES_X = ((1, 0), (-1, 0))
FACES_Y = ((0, 1), (0, -1))
E = 8
H = 2
C = 64
Z = 128
TAPS = 9
CHUNK = 2


def source_span(step):
    return pl.ds(H, E) if step == 0 else pl.ds(E if step > 0 else H, H)


def landing_span(step):
    return pl.ds(H, E) if step == 0 else pl.ds(0 if step > 0 else E + H, H)


def column(row):
    spread = jnp.broadcast_to(row, (C, C))
    on_diagonal = lax.broadcasted_iota(jnp.int32, (C, C), 0) == lax.broadcasted_iota(jnp.int32, (C, C), 1)
    return jnp.sum(jnp.where(on_diagonal, spread, 0.0), axis=1, keepdims=True)


def prepare_weight(held, ready):
    for c in range(3):
        rows = pl.ds(c * C, C)
        for pair in range(TAPS // 2):
            both = jnp.concatenate([held[(2 * pair) * 3 + c], held[(2 * pair + 1) * 3 + c]], axis=1)
            ready[rows, pl.ds(pair * 2 * C, 2 * C)] = both
        ready[rows, pl.ds((TAPS - 1) * C, C)] = held[(TAPS - 1) * 3 + c]


def conv_pair(src, ready, bias, spots, put):
    stacked = []
    for a in range(3):
        for b in range(3):
            stacked.append(jnp.concatenate([src[x + a, y + b] for x, y in spots], axis=1))
    sums = jnp.dot(ready[...], jnp.concatenate(stacked, axis=0), preferred_element_type=jnp.float32)
    lane = lax.broadcasted_iota(jnp.int32, (C, Z), 1)
    for half, (x, y) in enumerate(spots):
        part = sums[:, half * Z : (half + 1) * Z]
        before = jnp.where(lane == 0, 0.0, pltpu.roll(part[:C], 1, 1))
        after = jnp.where(lane == Z - 1, 0.0, pltpu.roll(part[2 * C :], Z - 1, 1))
        put(x, y, jnp.maximum(part[C : 2 * C] + before + after + bias, 0.0))


def remote_kernel(
    shape, feat_hbm, occ_hbm, w1_hbm, b1_hbm, w2_hbm, b2_hbm, wd_hbm, second_ref, wd_ref,
    feat, occ_ref, b_held, grid, first, w_held, w1, w2, wd_held, wide, mask_ref, bias_ref, copy_sem, send_sem, recv_sem,
):
    n_region, n_dev = shape
    region, dev = lax.axis_index("region"), lax.axis_index("dev")
    pairs = (
        (feat_hbm, feat),
        (occ_hbm, occ_ref),
        (w1_hbm, w_held.at[0]),
        (w2_hbm, w_held.at[1]),
        (wd_hbm, wd_held),
        (b1_hbm, b_held.at[0]),
        (b2_hbm, b_held.at[1]),
    )
    loads = [pltpu.make_async_copy(src, dst, copy_sem.at[k]) for k, (src, dst) in enumerate(pairs)]
    for load in loads:
        load.start()

    def there(dr, dd):
        r, d = region + dr, dev + dd
        return (r >= 0) & (r < n_region) & (d >= 0) & (d < n_dev)

    barrier = pltpu.get_barrier_semaphore()
    count = 0
    for dr, dd in CORNERS + FACES_X + FACES_Y:
        here = there(dr, dd)
        count = count + here.astype(jnp.int32)

        @pl.when(here)
        def _():
            pl.semaphore_signal(barrier, inc=1, device_id=(region + dr, dev + dd), device_id_type=MESH)

    made = []

    def transfer(dr, dd, src_x, dst_x):
        copy = pltpu.make_async_remote_copy(
            src_ref=grid.at[src_x, source_span(dd)],
            dst_ref=grid.at[dst_x, landing_span(dd)],
            send_sem=send_sem.at[len(made)],
            recv_sem=recv_sem.at[len(made)],
            device_id=(region + dr, dev + dd),
            device_id_type=MESH,
        )
        made.append((copy, there(dr, dd), there(-dr, -dd)))
        return made[-1]

    faces_x = [transfer(dr, dd, source_span(dr), landing_span(dr)) for dr, dd in FACES_X]
    low = [transfer(dr, dd, source_span(dr), landing_span(dr)) for dr, dd in CORNERS if dr > 0]
    chunks = []
    for x in range(H, H + E, CHUNK):
        chunks.append([transfer(dr, dd, pl.ds(x, CHUNK), pl.ds(x, CHUNK)) for dr, dd in FACES_Y])
    high = [transfer(dr, dd, source_span(dr), landing_span(dr)) for dr, dd in CORNERS if dr < 0]

    def arrived(group):
        for copy, _, comes in group:
            pl.when(comes)(copy.wait_recv)

    for dr, dd in CORNERS + FACES_X + FACES_Y:

        @pl.when(jnp.logical_not(there(-dr, -dd)))
        def _():
            nx, ny = (E if dr == 0 else H), (E if dd == 0 else H)
            grid[landing_span(dr), landing_span(dd)] = jnp.zeros((nx, ny, C, Z), jnp.bfloat16)

    loads[1].wait()
    bricks, devs = occ_ref.shape[1:]
    lanes = lax.broadcasted_iota(jnp.int32, (bricks, devs), 1)
    brick = lax.broadcasted_iota(jnp.int32, (bricks, Z), 0)
    voxel = lax.broadcasted_iota(jnp.int32, (bricks, Z), 1)
    span = Z // bricks
    inside = (voxel >= brick * span) & (voxel < (brick + 1) * span)
    for dr in (-1, 0, 1):
        valid = (region + dr >= 0) & (region + dr < n_region)
        held = occ_ref[jnp.clip(region + dr, 0, n_region - 1)].astype(jnp.float32)
        held = held * valid.astype(jnp.float32)
        for dd in (-1, 0, 1):
            level = jnp.sum(jnp.where(lanes == dev + dd, held, 0.0), axis=1, keepdims=True)
            mask_ref[dr + 1, dd + 1] = jnp.sum(jnp.where(inside, level, 0.0), axis=0, keepdims=True)

    mask = mask_ref[1, 1]
    loads[0].wait()
    for x in range(0, E, 2):
        slab = jnp.concatenate([feat[pl.ds(c * E * E + x * E, 2 * E), :] for c in range(C)], axis=0)
        blocks = jnp.swapaxes(slab.reshape(C, 2 * E, Z), 0, 1)
        blocks = jnp.where(mask[None] > 0, blocks, jnp.zeros_like(blocks))
        for k in range(2):
            grid[x + k + H, pl.ds(H, E)] = blocks[k * E : (k + 1) * E]

    pl.semaphore_wait(barrier, count)
    for group in [low] + chunks[:1] + [faces_x] + chunks[1:] + [high]:
        for copy, goes, _ in group:
            pl.when(goes)(copy.start)

    loads[2].wait()
    prepare_weight(w_held.at[0], w1)
    loads[3].wait()
    prepare_weight(w_held.at[1], w2)
    for k in range(2):
        loads[5 + k].wait()
        bias_ref[k] = jnp.broadcast_to(column(b_held[k]), (C, Z))
    loads[4].wait()
    wide[...] = wd_held[...].astype(jnp.float32)
    for c in range(2):
        for a in range(2):
            both = [wide[pl.ds(a * 4 + b * 2 + c, C, stride=8), :].astype(jnp.bfloat16) for b in range(2)]
            wd_ref[pl.ds(c * C, C), pl.ds(a * 2 * C, 2 * C)] = jnp.concatenate(both, axis=1)

    def side(at):
        return 0 if at == 0 else 2 if at == E + 1 else 1

    def put_first(x, y, value):
        first[x, y] = (value * mask_ref[side(x), side(y)]).astype(jnp.bfloat16)

    def put_second(x, y, value):
        second_ref[x, y] = (value * mask).astype(jnp.bfloat16)

    def one(x, y):
        conv_pair(grid, w1, bias_ref[0], ((x, y), (x, y + 1)), put_first)

    def two(x, y):
        conv_pair(first, w2, bias_ref[1], ((x, y), (x, y + 1)), put_second)

    for x in range(2, E):
        for y in range(2, E, 2):
            one(x, y)
    for x in range(2, E - 2):
        for y in range(2, E - 2, 2):
            two(x, y)
    arrived(faces_x)
    for x in (0, 1, E, E + 1):
        for y in range(2, E, 2):
            one(x, y)
    for x in (0, 1, E - 2, E - 1):
        for y in range(2, E - 2, 2):
            two(x, y)
    arrived(low)
    for k, group in enumerate(chunks + [high]):
        arrived(group)
        upto = H + CHUNK * (k + 1)
        for x in range(upto - CHUNK - 2, upto - 2):
            for y in (0, E):
                one(x, y)
        for x in range(max(upto - CHUNK - 4, 0), upto - 4):
            for y in (0, E - 2):
                two(x, y)
    for copy, goes, _ in made:
        pl.when(goes)(copy.wait_send)


def local_kernel(second_ref, wd_ref, bd_ref, skip_hbm, down_ref, slabs, narrow, copy_sem):
    copies = []
    for k, x in enumerate(range(0, E, 2)):
        slabs[k] = jnp.swapaxes(jnp.concatenate([second_ref[x], second_ref[x + 1]], axis=0), 0, 1)
        copy = pltpu.make_async_copy(slabs.at[k], skip_hbm.at[:, pl.ds(x * E, 2 * E), :], copy_sem.at[k])
        copy.start()
        copies.append(copy)

    lane_in = lax.broadcasted_iota(jnp.int32, (2 * Z, Z), 0)
    lane_out = lax.broadcasted_iota(jnp.int32, (2 * Z, Z), 1)
    keep = jnp.where(lane_in == 2 * lane_out, 1.0, 0.0).astype(jnp.bfloat16)
    bias = jnp.broadcast_to(column(bd_ref[...]), (C, 2 * Z))
    half = E // 2
    for x in range(half):
        for y in range(0, E, 4):
            stacked = [
                jnp.concatenate([second_ref[2 * x + a, y + 2 * k + b] for k in range(2)], axis=1)
                for a in range(2)
                for b in range(2)
            ]
            sums = jnp.dot(wd_ref[...], jnp.concatenate(stacked, axis=0), preferred_element_type=jnp.float32)
            moved = jnp.concatenate([pltpu.roll(sums[C:, k * Z : (k + 1) * Z], Z - 1, 1) for k in range(2)], axis=1)
            value = jnp.maximum(sums[:C] + moved + bias, 0.0).astype(jnp.bfloat16)
            narrow[y // 4, pl.ds(x, C, stride=half), :] = jnp.dot(value, keep, preferred_element_type=jnp.float32)
    for k in range(2):
        down_ref[:, :, pl.ds(k * Z, Z)] = narrow[k].reshape(C, half, Z).astype(jnp.bfloat16)
    for copy in copies:
        copy.wait()


def on_device(shape, features, occupancy, weight_one, bias_one, weight_two, bias_two, weight_down, bias_down):
    bf16, f32 = jnp.bfloat16, jnp.float32
    hbm = pl.BlockSpec(memory_space=pltpu.HBM)
    vmem = pl.BlockSpec(memory_space=pltpu.VMEM)
    rows = C * E * E
    held = [w.transpose(2, 3, 4, 0, 1).reshape(27, C, C) for w in (weight_one, weight_two)]
    n_copies = 6 + 2 * E // CHUNK
    operands = (
        features.reshape(rows, Z),
        occupancy.transpose(0, 2, 1),
        held[0],
        bias_one.reshape(1, C),
        held[1],
        bias_two.reshape(1, C),
        weight_down.transpose(0, 2, 3, 4, 1).reshape(8 * C, C),
    )
    second, wd = pl.pallas_call(
        functools.partial(remote_kernel, shape),
        out_shape=(jax.ShapeDtypeStruct((E, E, C, Z), bf16), jax.ShapeDtypeStruct((2 * C, 4 * C), bf16)),
        in_specs=[hbm] * len(operands),
        out_specs=(vmem, vmem),
        scratch_shapes=[
            pltpu.VMEM((rows, Z), bf16),
            pltpu.VMEM((shape[0], occupancy.shape[2], shape[1]), jnp.int32),
            pltpu.VMEM((2, 1, C), f32),
            pltpu.VMEM((E + 2 * H, E + 2 * H, C, Z), bf16),
            pltpu.VMEM((E + 2, E + 2, C, Z), bf16),
            pltpu.VMEM((2, 27, C, C), bf16),
            pltpu.VMEM((3 * C, TAPS * C), bf16),
            pltpu.VMEM((3 * C, TAPS * C), bf16),
            pltpu.VMEM((8 * C, C), bf16),
            pltpu.VMEM((8 * C, C), f32),
            pltpu.VMEM((3, 3, 1, Z), f32),
            pltpu.VMEM((2, C, Z), f32),
            pltpu.SemaphoreType.DMA((len(operands),)),
            pltpu.SemaphoreType.DMA((n_copies,)),
            pltpu.SemaphoreType.DMA((n_copies,)),
        ],
        compiler_params=pltpu.CompilerParams(
            collective_id=0, has_side_effects=True, vmem_limit_bytes=32 * 1024 * 1024
        ),
        name="halo_convs",
    )(*(pltpu.with_memory_space_constraint(operand, pltpu.HBM) for operand in operands))
    skip, down = pl.pallas_call(
        local_kernel,
        out_shape=(
            jax.ShapeDtypeStruct((C, E * E, Z), bf16),
            jax.ShapeDtypeStruct((C, E // 2, 2 * Z), bf16),
        ),
        in_specs=[vmem] * 3,
        out_specs=(hbm, vmem),
        scratch_shapes=[
            pltpu.VMEM((E // 2, C, 2 * E, Z), bf16),
            pltpu.VMEM((2, C * E // 2, Z), f32),
            pltpu.SemaphoreType.DMA((E // 2,)),
        ],
        compiler_params=pltpu.CompilerParams(vmem_limit_bytes=32 * 1024 * 1024),
        name="skip_and_down",
    )(second, wd, bias_down.reshape(1, C))
    return skip.reshape(C, E, E, Z), down


def solution(mesh):
    return jax.shard_map(
        functools.partial(on_device, (mesh.shape["region"], mesh.shape["dev"])),
        mesh=mesh,
        in_specs=(P(None, "region", "dev", None), P(), P(), P(), P(), P(), P(), P()),
        out_specs=(P(None, "region", "dev", None), P(None, "region", "dev")),
        check_vma=False,
    )
```

```python
import functools

import jax
import jax.numpy as jnp
from jax import lax
from jax.experimental import pallas as pl
from jax.experimental.pallas import tpu as pltpu
from jax.sharding import PartitionSpec as P

MESH = pl.DeviceIdType.MESH
FACES_X = ((1, 0), (-1, 0))
FACES_Y = ((0, 1), (0, -1))
CORNERS = ((1, 1), (1, -1), (-1, 1), (-1, -1))
DIRECT, PASSED = CORNERS[:2], CORNERS[2:]
E = 8
H = 2
C = 64
Z = 128
TAPS = 9
CHUNKS = ((0, 2), (2, 2), (4, 2), (6, 2))
SLABS = (0, 3, 1, 2)
SENDS = ("0", "near", "low", "far", "1", "2", "3")
TAKES = ("near", "0", "far", "low", "1", "2", "3", "high")


def source_span(step):
    return pl.ds(H, E) if step == 0 else pl.ds(E if step > 0 else H, H)


def landing_span(step):
    return pl.ds(H, E) if step == 0 else pl.ds(0 if step > 0 else E + H, H)


def column(row):
    spread = jnp.broadcast_to(row, (C, C))
    on_diagonal = lax.broadcasted_iota(jnp.int32, (C, C), 0) == lax.broadcasted_iota(jnp.int32, (C, C), 1)
    return jnp.sum(jnp.where(on_diagonal, spread, 0.0), axis=1, keepdims=True)


def prepare_weight(held, ready):
    for c in range(3):
        rows = pl.ds(c * C, C)
        for pair in range(TAPS // 2):
            both = jnp.concatenate([held[(2 * pair) * 3 + c], held[(2 * pair + 1) * 3 + c]], axis=1)
            ready[rows, pl.ds(pair * 2 * C, 2 * C)] = both
        ready[rows, pl.ds((TAPS - 1) * C, C)] = held[(TAPS - 1) * 3 + c]


def conv_pair(src, ready, bias, spots, put):
    stacked = []
    for a in range(3):
        for b in range(3):
            stacked.append(jnp.concatenate([src[x + a, y + b] for x, y in spots], axis=1))
    sums = jnp.dot(ready[...], jnp.concatenate(stacked, axis=0), preferred_element_type=jnp.float32)
    lane = lax.broadcasted_iota(jnp.int32, (C, Z), 1)
    for half, (x, y) in enumerate(spots):
        part = sums[:, half * Z : (half + 1) * Z]
        before = jnp.where(lane == 0, 0.0, pltpu.roll(part[:C], 1, 1))
        after = jnp.where(lane == Z - 1, 0.0, pltpu.roll(part[2 * C :], Z - 1, 1))
        put(x, y, jnp.maximum(part[C : 2 * C] + before + after + bias, 0.0))


def remote_kernel(
    shape, feat_hbm, occ_hbm, w1_hbm, b1_hbm, w2_hbm, b2_hbm, wd_hbm, bd_hbm, slab_ref, down_ref,
    feat, occ_ref, b_held, grid, first, second, w_held, w1, w2, wd_held, wide, wd, keep, narrow, mask_ref, bias_ref,
    copy_sem, send_sem, recv_sem,
):
    n_region, n_dev = shape
    region, dev = lax.axis_index("region"), lax.axis_index("dev")
    pairs = (
        (occ_hbm, occ_ref),
        (w1_hbm, w_held.at[0]),
        (w2_hbm, w_held.at[1]),
        (wd_hbm, wd_held),
        (b1_hbm, b_held.at[0]),
        (b2_hbm, b_held.at[1]),
        (bd_hbm, b_held.at[2]),
    )
    planes = []
    for k in range(E // 2):
        part = feat_hbm.at[:, pl.ds(2 * k * E, 2 * E), :]
        planes.append(pltpu.make_async_copy(part, feat.at[k], copy_sem.at[len(pairs) + k]))
    loads = [pltpu.make_async_copy(src, dst, copy_sem.at[k]) for k, (src, dst) in enumerate(pairs)]
    loads[0].start()
    for k in SLABS:
        planes[k].start()
    for load in loads[1:]:
        load.start()

    def there(dr, dd):
        r, d = region + dr, dev + dd
        return (r >= 0) & (r < n_region) & (d >= 0) & (d < n_dev)

    barrier = pltpu.get_barrier_semaphore()
    count = 0
    for dr, dd in FACES_Y + FACES_X + DIRECT:
        count = count + there(dr, dd).astype(jnp.int32)

        @pl.when(there(-dr, -dd))
        def _():
            pl.semaphore_signal(barrier, inc=1, device_id=(region - dr, dev - dd), device_id_type=MESH)

    made = []

    def transfer(to, src, dst, goes, comes):
        copy = pltpu.make_async_remote_copy(
            src_ref=grid.at[src],
            dst_ref=grid.at[dst],
            send_sem=send_sem.at[len(made)],
            recv_sem=recv_sem.at[len(made)],
            device_id=(region + to[0], dev + to[1]),
            device_id_type=MESH,
        )
        made.append((copy, goes, comes))
        return made[-1]

    def straight(dr, dd):
        src, dst = (source_span(dr), source_span(dd)), (landing_span(dr), landing_span(dd))
        return transfer((dr, dd), src, dst, there(dr, dd), there(-dr, -dd))

    def passed_on(dr, dd):
        src, dst = (source_span(dr), landing_span(dd)), (landing_span(dr), landing_span(dd))
        return transfer((dr, 0), src, dst, there(dr, 0) & there(dr, -dd) & there(0, -dd), there(-dr, -dd))

    groups = {"low": [straight(*way) for way in DIRECT], "high": [passed_on(*way) for way in PASSED]}
    for name, up, down in (("near", (E + 1, 1), (H, E + H)), ("far", (E, 0), (H + 1, E + H + 1))):
        groups[name] = []
        for dr, (src, dst) in ((1, up), (-1, down)):
            src, dst = (pl.ds(src, 1), pl.ds(H, E)), (pl.ds(dst, 1), pl.ds(H, E))
            groups[name].append(transfer((dr, 0), src, dst, there(dr, 0), there(-dr, 0)))
    for k, (first_x, planes_x) in enumerate(CHUNKS):
        groups[str(k)] = []
        x = pl.ds(H + first_x, planes_x)
        for dr, dd in FACES_Y:
            src, dst = (x, source_span(dd)), (x, landing_span(dd))
            groups[str(k)].append(transfer((dr, dd), src, dst, there(dr, dd), there(-dr, -dd)))

    def start(group):
        for copy, goes, _ in group:
            pl.when(goes)(copy.start)

    def arrived(group):
        for copy, _, comes in group:
            pl.when(comes)(copy.wait_recv)

    loads[0].wait()
    bricks, devs = occ_ref.shape[1:]
    lanes = lax.broadcasted_iota(jnp.int32, (bricks, devs), 1)
    brick = lax.broadcasted_iota(jnp.int32, (bricks, Z), 0)
    voxel = lax.broadcasted_iota(jnp.int32, (bricks, Z), 1)
    span = Z // bricks
    inside = (voxel >= brick * span) & (voxel < (brick + 1) * span)
    for dr in (-1, 0, 1):
        valid = (region + dr >= 0) & (region + dr < n_region)
        held = occ_ref[jnp.clip(region + dr, 0, n_region - 1)].astype(jnp.float32)
        held = held * valid.astype(jnp.float32)
        for dd in (-1, 0, 1):
            level = jnp.sum(jnp.where(lanes == dev + dd, held, 0.0), axis=1, keepdims=True)
            mask_ref[dr + 1, dd + 1] = jnp.sum(jnp.where(inside, level, 0.0), axis=0, keepdims=True)

    mask = mask_ref[1, 1]
    for k in SLABS:
        planes[k].wait()
        blocks = jnp.swapaxes(feat[k], 0, 1)
        blocks = jnp.where(mask[None] > 0, blocks, jnp.zeros_like(blocks))
        for h in range(2):
            grid[2 * k + h + H, pl.ds(H, E)] = blocks[h * E : (h + 1) * E]

    def side(at):
        return 0 if at == 0 else 2 if at == E + 1 else 1

    def put_first(x, y, value):
        first[x, y] = (value * mask_ref[side(x), side(y)]).astype(jnp.bfloat16)

    def put_second(x, y, value):
        second[x, y] = (value * mask).astype(jnp.bfloat16)

    def one(x, y):
        conv_pair(grid, w1, bias_ref[0], ((x, y), (x, y + 1)), put_first)

    def two(x, y):
        conv_pair(first, w2, bias_ref[1], ((x, y), (x, y + 1)), put_second)

    def finish(k):
        x = 2 * k
        slab_ref[k] = jnp.swapaxes(jnp.concatenate([second[x], second[x + 1]], axis=0), 0, 1)
        stacked = []
        for a in range(2):
            for b in range(2):
                stacked.append(jnp.concatenate([second[x + a, y + b] for y in range(0, E, 2)], axis=1))
        sums = jnp.dot(wd[...], jnp.concatenate(stacked, axis=0), preferred_element_type=jnp.float32)
        lowered = []
        for y in range(E // 2):
            part = sums[:, y * Z : (y + 1) * Z]
            value = part[:C] + pltpu.roll(part[C:], Z - 1, 1) + bias_ref[2]
            lowered.append(jnp.maximum(value, 0.0).astype(jnp.bfloat16))
        for h in range(2):
            both = jnp.concatenate(lowered[2 * h : 2 * h + 2], axis=1)
            kept = jnp.dot(both, keep[...], preferred_element_type=jnp.float32)
            narrow[h, pl.ds(k, C, stride=E // 2), :] = kept

    pl.semaphore_wait(barrier, count)
    for name in SENDS:
        start(groups[name])

    for dr, dd in CORNERS + FACES_X + FACES_Y:

        @pl.when(jnp.logical_not(there(-dr, -dd)))
        def _():
            nx, ny = (E if dr == 0 else H), (E if dd == 0 else H)
            grid[landing_span(dr), landing_span(dd)] = jnp.zeros((nx, ny, C, Z), jnp.bfloat16)

    loads[1].wait()
    prepare_weight(w_held.at[0], w1)
    for k in range(3):
        loads[4 + k].wait()
        bias_ref[k] = jnp.broadcast_to(column(b_held[k]), (C, Z))
    for x in range(2, E):
        for y in range(2, E, 2):
            one(x, y)
    loads[2].wait()
    prepare_weight(w_held.at[1], w2)
    loads[3].wait()
    wide[...] = wd_held[...].astype(jnp.float32)
    for c in range(2):
        for a in range(2):
            both = [wide[pl.ds(a * 4 + b * 2 + c, C, stride=8), :].astype(jnp.bfloat16) for b in range(2)]
            wd[pl.ds(c * C, C), pl.ds(a * 2 * C, 2 * C)] = jnp.concatenate(both, axis=1)
    lane_in = lax.broadcasted_iota(jnp.int32, (2 * Z, Z), 0)
    lane_out = lax.broadcasted_iota(jnp.int32, (2 * Z, Z), 1)
    keep[...] = jnp.where(lane_in == 2 * lane_out, 1.0, 0.0).astype(jnp.bfloat16)

    for x in range(2, E - 2):
        for y in range(2, E - 2, 2):
            two(x, y)

    landed, landed_rim = set(range(H, E + H)), set()
    one_middle, one_rim = set(range(2, E)), set()
    two_middle, two_rim = set(range(2, E - 2)), set()

    def advance():
        for x in range(E + 2):
            if x not in one_middle and {x, x + 1, x + 2} <= landed:
                for y in range(2, E, 2):
                    one(x, y)
                one_middle.add(x)
        for x in range(E):
            if x not in two_middle and {x, x + 1, x + 2} <= one_middle:
                for y in range(2, E - 2, 2):
                    two(x, y)
                two_middle.add(x)
        for x in range(E + 2):
            if x not in one_rim and {x, x + 1, x + 2} <= landed_rim:
                for y in (0, E):
                    one(x, y)
                one_rim.add(x)
        for x in range(E):
            if x not in two_rim and {x, x + 1, x + 2} <= one_rim & one_middle:
                for y in (0, E - 2):
                    two(x, y)
                two_rim.add(x)
                if x ^ 1 in two_rim:
                    finish(x // 2)

    for name in TAKES:
        arrived(groups[name])
        if name == "near":
            landed.update((1, E + H))
        elif name == "far":
            landed.update((0, E + H + 1))
        elif name == "low":
            landed_rim.update(range(H))
        elif name == "high":
            landed_rim.update(range(E + H, E + 2 * H))
        else:
            first_x, planes_x = CHUNKS[int(name)]
            landed_rim.update(range(H + first_x, H + first_x + planes_x))
            if first_x == 0:
                start(groups["high"])
        advance()
    for k in range(2):
        down_ref[:, :, pl.ds(k * Z, Z)] = narrow[k].reshape(C, E // 2, Z).astype(jnp.bfloat16)
    for copy, goes, _ in made:
        pl.when(goes)(copy.wait_send)


def local_kernel(slab_ref, down_in, skip_hbm, down_hbm, copy_sem):
    copies = [pltpu.make_async_copy(down_in, down_hbm, copy_sem.at[E // 2])]
    for k in range(E // 2):
        copies.append(pltpu.make_async_copy(slab_ref.at[k], skip_hbm.at[:, pl.ds(2 * k * E, 2 * E), :], copy_sem.at[k]))
    for copy in copies:
        copy.start()
    for copy in copies:
        copy.wait()


def on_device(shape, features, occupancy, weight_one, bias_one, weight_two, bias_two, weight_down, bias_down):
    bf16, f32 = jnp.bfloat16, jnp.float32
    hbm = pl.BlockSpec(memory_space=pltpu.HBM)
    vmem = pl.BlockSpec(memory_space=pltpu.VMEM)
    held = [w.transpose(2, 3, 4, 0, 1).reshape(27, C, C) for w in (weight_one, weight_two)]
    n_copies = 2 * len(CHUNKS) + 8
    n_loads = 7 + E // 2
    operands = (
        features.reshape(C, E * E, Z),
        occupancy.transpose(0, 2, 1),
        held[0],
        bias_one.reshape(1, C),
        held[1],
        bias_two.reshape(1, C),
        weight_down.transpose(0, 2, 3, 4, 1).reshape(8 * C, C),
        bias_down.reshape(1, C),
    )
    slabs, down = pl.pallas_call(
        functools.partial(remote_kernel, shape),
        out_shape=(
            jax.ShapeDtypeStruct((E // 2, C, 2 * E, Z), bf16),
            jax.ShapeDtypeStruct((C, E // 2, 2 * Z), bf16),
        ),
        in_specs=[hbm] * len(operands),
        out_specs=(vmem, vmem),
        scratch_shapes=[
            pltpu.VMEM((E // 2, C, 2 * E, Z), bf16),
            pltpu.VMEM((shape[0], occupancy.shape[2], shape[1]), jnp.int32),
            pltpu.VMEM((3, 1, C), f32),
            pltpu.VMEM((E + 2 * H, E + 2 * H, C, Z), bf16),
            pltpu.VMEM((E + 2, E + 2, C, Z), bf16),
            pltpu.VMEM((E, E, C, Z), bf16),
            pltpu.VMEM((2, 27, C, C), bf16),
            pltpu.VMEM((3 * C, TAPS * C), bf16),
            pltpu.VMEM((3 * C, TAPS * C), bf16),
            pltpu.VMEM((8 * C, C), bf16),
            pltpu.VMEM((8 * C, C), f32),
            pltpu.VMEM((2 * C, 4 * C), bf16),
            pltpu.VMEM((2 * Z, Z), bf16),
            pltpu.VMEM((2, C * E // 2, Z), f32),
            pltpu.VMEM((3, 3, 1, Z), f32),
            pltpu.VMEM((3, C, Z), f32),
            pltpu.SemaphoreType.DMA((n_loads,)),
            pltpu.SemaphoreType.DMA((n_copies,)),
            pltpu.SemaphoreType.DMA((n_copies,)),
        ],
        compiler_params=pltpu.CompilerParams(
            collective_id=0, has_side_effects=True, vmem_limit_bytes=32 * 1024 * 1024
        ),
        name="halo_convs",
    )(*(pltpu.with_memory_space_constraint(operand, pltpu.HBM) for operand in operands))
    skip, down = pl.pallas_call(
        local_kernel,
        out_shape=(
            jax.ShapeDtypeStruct((C, E * E, Z), bf16),
            jax.ShapeDtypeStruct((C, E // 2, 2 * Z), bf16),
        ),
        in_specs=[vmem] * 2,
        out_specs=(hbm, hbm),
        scratch_shapes=[pltpu.SemaphoreType.DMA((E // 2 + 1,))],
        compiler_params=pltpu.CompilerParams(vmem_limit_bytes=32 * 1024 * 1024),
        name="copy_out",
    )(slabs, down)
    return skip.reshape(C, E, E, Z), down


def solution(mesh):
    return jax.shard_map(
        functools.partial(on_device, (mesh.shape["region"], mesh.shape["dev"])),
        mesh=mesh,
        in_specs=(P(None, "region", "dev", None), P(), P(), P(), P(), P(), P(), P()),
        out_specs=(P(None, "region", "dev", None), P(None, "region", "dev")),
        check_vma=False,
    )
```

```python
import functools

import jax
import jax.numpy as jnp
from jax import lax
from jax.experimental import pallas as pl
from jax.experimental.pallas import tpu as pltpu
from jax.sharding import PartitionSpec as P

MESH = pl.DeviceIdType.MESH
FACES_X = ((1, 0), (-1, 0))
FACES_Y = ((0, 1), (0, -1))
CORNERS = ((1, 1), (1, -1), (-1, 1), (-1, -1))
DIRECT, PASSED = CORNERS[:2], CORNERS[2:]
E = 8
H = 2
C = 64
Z = 128
TAPS = 9
CHUNKS = ((0, 2), (2, 2), (4, 2), (6, 2))
SLABS = (0, 3, 1, 2)
SENDS = ("0", "near", "low", "far", "1", "2", "3")
TAKES = ("0", "near", "far", "low", "1", "2", "3", "high")


def source_span(step):
    return pl.ds(H, E) if step == 0 else pl.ds(E if step > 0 else H, H)


def landing_span(step):
    return pl.ds(H, E) if step == 0 else pl.ds(0 if step > 0 else E + H, H)


def column(row):
    spread = jnp.broadcast_to(row, (C, C))
    on_diagonal = lax.broadcasted_iota(jnp.int32, (C, C), 0) == lax.broadcasted_iota(jnp.int32, (C, C), 1)
    return jnp.sum(jnp.where(on_diagonal, spread, 0.0), axis=1, keepdims=True)


def prepare_weight(held, ready):
    for c in range(3):
        rows = pl.ds(c * C, C)
        for pair in range(TAPS // 2):
            both = jnp.concatenate([held[(2 * pair) * 3 + c], held[(2 * pair + 1) * 3 + c]], axis=1)
            ready[rows, pl.ds(pair * 2 * C, 2 * C)] = both
        ready[rows, pl.ds((TAPS - 1) * C, C)] = held[(TAPS - 1) * 3 + c]


def conv_pair(src, ready, bias, spots, put):
    stacked = []
    for a in range(3):
        for b in range(3):
            stacked.append(jnp.concatenate([src[x + a, y + b] for x, y in spots], axis=1))
    sums = jnp.dot(ready[...], jnp.concatenate(stacked, axis=0), preferred_element_type=jnp.float32)
    lane = lax.broadcasted_iota(jnp.int32, (C, Z), 1)
    for half, (x, y) in enumerate(spots):
        part = sums[:, half * Z : (half + 1) * Z]
        before = jnp.where(lane == 0, 0.0, pltpu.roll(part[:C], 1, 1))
        after = jnp.where(lane == Z - 1, 0.0, pltpu.roll(part[2 * C :], Z - 1, 1))
        put(x, y, jnp.maximum(part[C : 2 * C] + before + after + bias, 0.0))


def remote_kernel(
    shape, feat_hbm, occ_hbm, w1_hbm, b1_hbm, w2_hbm, b2_hbm, wd_hbm, bd_hbm, slab_ref, down_ref,
    feat, occ_ref, b_held, grid, first, second, w_held, w1, w2, wd_held, wide, wd, keep, narrow, mask_ref, bias_ref,
    copy_sem, send_sem, recv_sem,
):
    n_region, n_dev = shape
    region, dev = lax.axis_index("region"), lax.axis_index("dev")
    pairs = (
        (occ_hbm, occ_ref),
        (w1_hbm, w_held.at[0]),
        (w2_hbm, w_held.at[1]),
        (wd_hbm, wd_held),
        (b1_hbm, b_held.at[0]),
        (b2_hbm, b_held.at[1]),
        (bd_hbm, b_held.at[2]),
    )
    planes = []
    for k in range(E // 2):
        part = feat_hbm.at[:, pl.ds(2 * k * E, 2 * E), :]
        planes.append(pltpu.make_async_copy(part, feat.at[k], copy_sem.at[len(pairs) + k]))
    loads = [pltpu.make_async_copy(src, dst, copy_sem.at[k]) for k, (src, dst) in enumerate(pairs)]
    loads[0].start()
    for k in SLABS:
        planes[k].start()
    for load in loads[1:]:
        load.start()

    def there(dr, dd):
        r, d = region + dr, dev + dd
        return (r >= 0) & (r < n_region) & (d >= 0) & (d < n_dev)

    barrier = pltpu.get_barrier_semaphore()
    count = 0
    for dr, dd in FACES_Y + FACES_X + DIRECT:
        count = count + there(dr, dd).astype(jnp.int32)

        @pl.when(there(-dr, -dd))
        def _():
            pl.semaphore_signal(barrier, inc=1, device_id=(region - dr, dev - dd), device_id_type=MESH)

    made = []

    def transfer(to, src, dst, goes, comes):
        copy = pltpu.make_async_remote_copy(
            src_ref=grid.at[src],
            dst_ref=grid.at[dst],
            send_sem=send_sem.at[len(made)],
            recv_sem=recv_sem.at[len(made)],
            device_id=(region + to[0], dev + to[1]),
            device_id_type=MESH,
        )
        made.append((copy, goes, comes))
        return made[-1]

    def straight(dr, dd):
        src, dst = (source_span(dr), source_span(dd)), (landing_span(dr), landing_span(dd))
        return transfer((dr, dd), src, dst, there(dr, dd), there(-dr, -dd))

    def passed_on(dr, dd):
        src, dst = (source_span(dr), landing_span(dd)), (landing_span(dr), landing_span(dd))
        return transfer((dr, 0), src, dst, there(dr, 0) & there(dr, -dd) & there(0, -dd), there(-dr, -dd))

    groups = {"low": [straight(*way) for way in DIRECT], "high": [passed_on(*way) for way in PASSED]}
    for name, up, down in (("near", (E + 1, 1), (H, E + H)), ("far", (E, 0), (H + 1, E + H + 1))):
        groups[name] = []
        for dr, (src, dst) in ((1, up), (-1, down)):
            src, dst = (pl.ds(src, 1), pl.ds(H, E)), (pl.ds(dst, 1), pl.ds(H, E))
            groups[name].append(transfer((dr, 0), src, dst, there(dr, 0), there(-dr, 0)))
    for k, (first_x, planes_x) in enumerate(CHUNKS):
        groups[str(k)] = []
        x = pl.ds(H + first_x, planes_x)
        for dr, dd in FACES_Y:
            src, dst = (x, source_span(dd)), (x, landing_span(dd))
            groups[str(k)].append(transfer((dr, dd), src, dst, there(dr, dd), there(-dr, -dd)))

    def start(group):
        for copy, goes, _ in group:
            pl.when(goes)(copy.start)

    def arrived(group):
        for copy, _, comes in group:
            pl.when(comes)(copy.wait_recv)

    loads[0].wait()
    bricks, devs = occ_ref.shape[1:]
    lanes = lax.broadcasted_iota(jnp.int32, (bricks, devs), 1)
    brick = lax.broadcasted_iota(jnp.int32, (bricks, Z), 0)
    voxel = lax.broadcasted_iota(jnp.int32, (bricks, Z), 1)
    span = Z // bricks
    inside = (voxel >= brick * span) & (voxel < (brick + 1) * span)
    for dr in (-1, 0, 1):
        valid = (region + dr >= 0) & (region + dr < n_region)
        held = occ_ref[jnp.clip(region + dr, 0, n_region - 1)].astype(jnp.float32)
        held = held * valid.astype(jnp.float32)
        for dd in (-1, 0, 1):
            level = jnp.sum(jnp.where(lanes == dev + dd, held, 0.0), axis=1, keepdims=True)
            mask_ref[dr + 1, dd + 1] = jnp.sum(jnp.where(inside, level, 0.0), axis=0, keepdims=True)

    mask = mask_ref[1, 1]
    for k in SLABS:
        planes[k].wait()
        blocks = jnp.swapaxes(feat[k], 0, 1)
        blocks = jnp.where(mask[None] > 0, blocks, jnp.zeros_like(blocks))
        for h in range(2):
            grid[2 * k + h + H, pl.ds(H, E)] = blocks[h * E : (h + 1) * E]

    def side(at):
        return 0 if at == 0 else 2 if at == E + 1 else 1

    def put_first(x, y, value):
        first[x, y] = (value * mask_ref[side(x), side(y)]).astype(jnp.bfloat16)

    def put_second(x, y, value):
        second[x, y] = (value * mask).astype(jnp.bfloat16)

    def one(x, y):
        conv_pair(grid, w1, bias_ref[0], ((x, y), (x, y + 1)), put_first)

    def two(x, y):
        conv_pair(first, w2, bias_ref[1], ((x, y), (x, y + 1)), put_second)

    def lower(k):
        x = 2 * k
        slab_ref[k] = jnp.swapaxes(jnp.concatenate([second[x], second[x + 1]], axis=0), 0, 1)
        stacked = []
        for a in range(2):
            for b in range(2):
                stacked.append(jnp.concatenate([second[x + a, y + b] for y in range(0, E, 2)], axis=1))
        sums = jnp.dot(wd[...], jnp.concatenate(stacked, axis=0), preferred_element_type=jnp.float32)
        lowered = []
        for y in range(E // 2):
            part = sums[:, y * Z : (y + 1) * Z]
            value = part[:C] + pltpu.roll(part[C:], Z - 1, 1) + bias_ref[2]
            lowered.append(jnp.maximum(value, 0.0).astype(jnp.bfloat16))
        return lowered

    def thin(k, lowered):
        for h in range(2):
            both = jnp.concatenate(lowered[2 * h : 2 * h + 2], axis=1)
            kept = jnp.dot(both, keep[...], preferred_element_type=jnp.float32)
            narrow[h, pl.ds(k, C, stride=E // 2), :] = kept

    pl.semaphore_wait(barrier, count)
    for name in SENDS:
        start(groups[name])

    for dr, dd in CORNERS + FACES_X + FACES_Y:

        @pl.when(jnp.logical_not(there(-dr, -dd)))
        def _():
            nx, ny = (E if dr == 0 else H), (E if dd == 0 else H)
            grid[landing_span(dr), landing_span(dd)] = jnp.zeros((nx, ny, C, Z), jnp.bfloat16)

    loads[1].wait()
    prepare_weight(w_held.at[0], w1)
    for k in range(3):
        loads[4 + k].wait()
        bias_ref[k] = jnp.broadcast_to(column(b_held[k]), (C, Z))
    for x in range(2, E):
        for y in range(2, E, 2):
            one(x, y)
    loads[2].wait()
    prepare_weight(w_held.at[1], w2)
    loads[3].wait()
    wide[...] = wd_held[...].astype(jnp.float32)
    for c in range(2):
        for a in range(2):
            both = [wide[pl.ds(a * 4 + b * 2 + c, C, stride=8), :].astype(jnp.bfloat16) for b in range(2)]
            wd[pl.ds(c * C, C), pl.ds(a * 2 * C, 2 * C)] = jnp.concatenate(both, axis=1)
    lane_in = lax.broadcasted_iota(jnp.int32, (2 * Z, Z), 0)
    lane_out = lax.broadcasted_iota(jnp.int32, (2 * Z, Z), 1)
    keep[...] = jnp.where(lane_in == 2 * lane_out, 1.0, 0.0).astype(jnp.bfloat16)

    for x in range(2, E - 2):
        for y in range(2, E - 2, 2):
            two(x, y)

    landed, landed_rim = set(range(H, E + H)), set()
    one_middle, one_rim = set(range(2, E)), set()
    two_middle, two_rim = set(range(2, E - 2)), set()

    complete = []

    def advance(last):
        lowered = [(k, lower(k)) for k in complete]
        complete.clear()
        for x in range(E + 2):
            if x not in one_middle and {x, x + 1, x + 2} <= landed:
                for y in range(2, E, 2):
                    one(x, y)
                one_middle.add(x)
        for x in range(E + 2):
            if x not in one_rim and {x, x + 1, x + 2} <= landed_rim:
                for y in (0, E):
                    one(x, y)
                one_rim.add(x)
        for k, planes_k in lowered:
            thin(k, planes_k)
        for x in range(E):
            if x not in two_middle and {x, x + 1, x + 2} <= one_middle:
                for y in range(2, E - 2, 2):
                    two(x, y)
                two_middle.add(x)
        for x in range(E):
            if x not in two_rim and {x, x + 1, x + 2} <= one_rim & one_middle:
                for y in (0, E - 2):
                    two(x, y)
                two_rim.add(x)
                if x ^ 1 in two_rim:
                    complete.append(x // 2)
        if last:
            for k, planes_k in [(k, lower(k)) for k in complete]:
                thin(k, planes_k)

    for name in TAKES:
        arrived(groups[name])
        if name == "near":
            landed.update((1, E + H))
        elif name == "far":
            landed.update((0, E + H + 1))
        elif name == "low":
            landed_rim.update(range(H))
        elif name == "high":
            landed_rim.update(range(E + H, E + 2 * H))
        else:
            first_x, planes_x = CHUNKS[int(name)]
            landed_rim.update(range(H + first_x, H + first_x + planes_x))
            if first_x == 0:
                start(groups["high"])
        if name != "3":
            advance(name == TAKES[-1])
    for k in range(2):
        down_ref[:, :, pl.ds(k * Z, Z)] = narrow[k].reshape(C, E // 2, Z).astype(jnp.bfloat16)
    for copy, goes, _ in made:
        pl.when(goes)(copy.wait_send)


def local_kernel(slab_ref, down_in, skip_hbm, down_hbm, copy_sem):
    copies = [pltpu.make_async_copy(down_in, down_hbm, copy_sem.at[E // 2])]
    for k in range(E // 2):
        copies.append(pltpu.make_async_copy(slab_ref.at[k], skip_hbm.at[:, pl.ds(2 * k * E, 2 * E), :], copy_sem.at[k]))
    for copy in copies:
        copy.start()
    for copy in copies:
        copy.wait()


def on_device(shape, features, occupancy, weight_one, bias_one, weight_two, bias_two, weight_down, bias_down):
    bf16, f32 = jnp.bfloat16, jnp.float32
    hbm = pl.BlockSpec(memory_space=pltpu.HBM)
    vmem = pl.BlockSpec(memory_space=pltpu.VMEM)
    held = [w.transpose(2, 3, 4, 0, 1).reshape(27, C, C) for w in (weight_one, weight_two)]
    n_copies = 2 * len(CHUNKS) + 8
    n_loads = 7 + E // 2
    operands = (
        features.reshape(C, E * E, Z),
        occupancy.transpose(0, 2, 1),
        held[0],
        bias_one.reshape(1, C),
        held[1],
        bias_two.reshape(1, C),
        weight_down.transpose(0, 2, 3, 4, 1).reshape(8 * C, C),
        bias_down.reshape(1, C),
    )
    slabs, down = pl.pallas_call(
        functools.partial(remote_kernel, shape),
        out_shape=(
            jax.ShapeDtypeStruct((E // 2, C, 2 * E, Z), bf16),
            jax.ShapeDtypeStruct((C, E // 2, 2 * Z), bf16),
        ),
        in_specs=[hbm] * len(operands),
        out_specs=(vmem, vmem),
        scratch_shapes=[
            pltpu.VMEM((E // 2, C, 2 * E, Z), bf16),
            pltpu.VMEM((shape[0], occupancy.shape[2], shape[1]), jnp.int32),
            pltpu.VMEM((3, 1, C), f32),
            pltpu.VMEM((E + 2 * H, E + 2 * H, C, Z), bf16),
            pltpu.VMEM((E + 2, E + 2, C, Z), bf16),
            pltpu.VMEM((E, E, C, Z), bf16),
            pltpu.VMEM((2, 27, C, C), bf16),
            pltpu.VMEM((3 * C, TAPS * C), bf16),
            pltpu.VMEM((3 * C, TAPS * C), bf16),
            pltpu.VMEM((8 * C, C), bf16),
            pltpu.VMEM((8 * C, C), f32),
            pltpu.VMEM((2 * C, 4 * C), bf16),
            pltpu.VMEM((2 * Z, Z), bf16),
            pltpu.VMEM((2, C * E // 2, Z), f32),
            pltpu.VMEM((3, 3, 1, Z), f32),
            pltpu.VMEM((3, C, Z), f32),
            pltpu.SemaphoreType.DMA((n_loads,)),
            pltpu.SemaphoreType.DMA((n_copies,)),
            pltpu.SemaphoreType.DMA((n_copies,)),
        ],
        compiler_params=pltpu.CompilerParams(
            collective_id=0, has_side_effects=True, vmem_limit_bytes=32 * 1024 * 1024
        ),
        name="halo_convs",
    )(*(pltpu.with_memory_space_constraint(operand, pltpu.HBM) for operand in operands))
    skip, down = pl.pallas_call(
        local_kernel,
        out_shape=(
            jax.ShapeDtypeStruct((C, E * E, Z), bf16),
            jax.ShapeDtypeStruct((C, E // 2, 2 * Z), bf16),
        ),
        in_specs=[vmem] * 2,
        out_specs=(hbm, hbm),
        scratch_shapes=[pltpu.SemaphoreType.DMA((E // 2 + 1,))],
        compiler_params=pltpu.CompilerParams(vmem_limit_bytes=32 * 1024 * 1024),
        name="copy_out",
    )(slabs, down)
    return skip.reshape(C, E, E, Z), down


def solution(mesh):
    return jax.shard_map(
        functools.partial(on_device, (mesh.shape["region"], mesh.shape["dev"])),
        mesh=mesh,
        in_specs=(P(None, "region", "dev", None), P(), P(), P(), P(), P(), P(), P()),
        out_specs=(P(None, "region", "dev", None), P(None, "region", "dev")),
        check_vma=False,
    )
```

```python
import functools

import jax
import jax.numpy as jnp
from jax import lax
from jax.experimental import pallas as pl
from jax.experimental.pallas import tpu as pltpu
from jax.sharding import PartitionSpec as P

MESH = pl.DeviceIdType.MESH
FACES_X = ((1, 0), (-1, 0))
FACES_Y = ((0, 1), (0, -1))
CORNERS = ((1, 1), (1, -1), (-1, 1), (-1, -1))
DIRECT, PASSED = CORNERS[:2], CORNERS[2:]
E = 8
H = 2
C = 64
Z = 128
TAPS = 9
CHUNKS = ((0, 2), (2, 2), (4, 2), (6, 2))
SLABS = (0, 3, 1, 2)
SENDS = ("0", "near", "low", "far", "1", "2", "3")
TAKES = ("0", "near", "far", "low", "1", "2", "3", "high")


def source_span(step):
    return pl.ds(H, E) if step == 0 else pl.ds(E if step > 0 else H, H)


def landing_span(step):
    return pl.ds(H, E) if step == 0 else pl.ds(0 if step > 0 else E + H, H)


def column(row):
    spread = jnp.broadcast_to(row, (C, C))
    on_diagonal = lax.broadcasted_iota(jnp.int32, (C, C), 0) == lax.broadcasted_iota(jnp.int32, (C, C), 1)
    return jnp.sum(jnp.where(on_diagonal, spread, 0.0), axis=1, keepdims=True)


def prepare_weight(held, ready):
    for c in range(3):
        rows = pl.ds(c * C, C)
        for pair in range(TAPS // 2):
            both = jnp.concatenate([held[(2 * pair) * 3 + c], held[(2 * pair + 1) * 3 + c]], axis=1)
            ready[rows, pl.ds(pair * 2 * C, 2 * C)] = both
        ready[rows, pl.ds((TAPS - 1) * C, C)] = held[(TAPS - 1) * 3 + c]


def conv_pair(src, ready, bias, spots, put):
    stacked = []
    for a in range(3):
        for b in range(3):
            stacked.append(jnp.concatenate([src[x + a, y + b] for x, y in spots], axis=1))
    sums = jnp.dot(ready[...], jnp.concatenate(stacked, axis=0), preferred_element_type=jnp.float32)
    lane = lax.broadcasted_iota(jnp.int32, (C, Z), 1)
    for half, (x, y) in enumerate(spots):
        part = sums[:, half * Z : (half + 1) * Z]
        before = jnp.where(lane == 0, 0.0, pltpu.roll(part[:C], 1, 1))
        after = jnp.where(lane == Z - 1, 0.0, pltpu.roll(part[2 * C :], Z - 1, 1))
        put(x, y, jnp.maximum(part[C : 2 * C] + before + after + bias, 0.0))


def remote_kernel(
    shape, feat_hbm, occ_hbm, w1_hbm, b1_hbm, w2_hbm, b2_hbm, wd_hbm, bd_hbm, slab_ref, down_ref,
    feat, occ_ref, b_held, grid, first, second, w_held, w1, w2, wd_held, wide, wd, keep, narrow, mask_ref, bias_ref,
    copy_sem, send_sem, recv_sem,
):
    n_region, n_dev = shape
    region, dev = lax.axis_index("region"), lax.axis_index("dev")
    pairs = (
        (occ_hbm, occ_ref),
        (w1_hbm, w_held.at[0]),
        (w2_hbm, w_held.at[1]),
        (wd_hbm, wd_held),
        (b1_hbm, b_held.at[0]),
        (b2_hbm, b_held.at[1]),
        (bd_hbm, b_held.at[2]),
    )
    planes = []
    for k in range(E // 2):
        part = feat_hbm.at[:, pl.ds(2 * k * E, 2 * E), :]
        planes.append(pltpu.make_async_copy(part, feat.at[k], copy_sem.at[len(pairs) + k]))
    loads = [pltpu.make_async_copy(src, dst, copy_sem.at[k]) for k, (src, dst) in enumerate(pairs)]
    loads[0].start()
    for k in SLABS:
        planes[k].start()
    for load in loads[1:]:
        load.start()

    def there(dr, dd):
        r, d = region + dr, dev + dd
        return (r >= 0) & (r < n_region) & (d >= 0) & (d < n_dev)

    barrier = pltpu.get_barrier_semaphore()
    count = 0
    for dr, dd in FACES_Y + FACES_X + DIRECT:
        count = count + there(dr, dd).astype(jnp.int32)

        @pl.when(there(-dr, -dd))
        def _():
            pl.semaphore_signal(barrier, inc=1, device_id=(region - dr, dev - dd), device_id_type=MESH)

    made = []

    def transfer(to, src, dst, goes, comes):
        copy = pltpu.make_async_remote_copy(
            src_ref=grid.at[src],
            dst_ref=grid.at[dst],
            send_sem=send_sem.at[len(made)],
            recv_sem=recv_sem.at[len(made)],
            device_id=(region + to[0], dev + to[1]),
            device_id_type=MESH,
        )
        made.append((copy, goes, comes))
        return made[-1]

    def straight(dr, dd):
        src, dst = (source_span(dr), source_span(dd)), (landing_span(dr), landing_span(dd))
        return transfer((dr, dd), src, dst, there(dr, dd), there(-dr, -dd))

    def passed_on(dr, dd):
        src, dst = (source_span(dr), landing_span(dd)), (landing_span(dr), landing_span(dd))
        return transfer((dr, 0), src, dst, there(dr, 0) & there(dr, -dd) & there(0, -dd), there(-dr, -dd))

    groups = {"low": [straight(*way) for way in DIRECT], "high": [passed_on(*way) for way in PASSED]}
    for name, up, down in (("near", (E + 1, 1), (H, E + H)), ("far", (E, 0), (H + 1, E + H + 1))):
        groups[name] = []
        for dr, (src, dst) in ((1, up), (-1, down)):
            src, dst = (pl.ds(src, 1), pl.ds(H, E)), (pl.ds(dst, 1), pl.ds(H, E))
            groups[name].append(transfer((dr, 0), src, dst, there(dr, 0), there(-dr, 0)))
    for k, (first_x, planes_x) in enumerate(CHUNKS):
        groups[str(k)] = []
        x = pl.ds(H + first_x, planes_x)
        for dr, dd in FACES_Y:
            src, dst = (x, source_span(dd)), (x, landing_span(dd))
            groups[str(k)].append(transfer((dr, dd), src, dst, there(dr, dd), there(-dr, -dd)))

    def start(group):
        for copy, goes, _ in group:
            pl.when(goes)(copy.start)

    def arrived(group):
        for copy, _, comes in group:
            pl.when(comes)(copy.wait_recv)

    loads[0].wait()
    bricks, devs = occ_ref.shape[1:]
    lanes = lax.broadcasted_iota(jnp.int32, (bricks, devs), 1)
    brick = lax.broadcasted_iota(jnp.int32, (bricks, Z), 0)
    voxel = lax.broadcasted_iota(jnp.int32, (bricks, Z), 1)
    span = Z // bricks
    inside = (voxel >= brick * span) & (voxel < (brick + 1) * span)
    for dr in (-1, 0, 1):
        valid = (region + dr >= 0) & (region + dr < n_region)
        held = occ_ref[jnp.clip(region + dr, 0, n_region - 1)].astype(jnp.float32)
        held = held * valid.astype(jnp.float32)
        for dd in (-1, 0, 1):
            level = jnp.sum(jnp.where(lanes == dev + dd, held, 0.0), axis=1, keepdims=True)
            mask_ref[dr + 1, dd + 1] = jnp.sum(jnp.where(inside, level, 0.0), axis=0, keepdims=True)

    mask = mask_ref[1, 1]
    for k in SLABS:
        planes[k].wait()
        blocks = jnp.swapaxes(feat[k], 0, 1)
        blocks = jnp.where(mask[None] > 0, blocks, jnp.zeros_like(blocks))
        for h in range(2):
            grid[2 * k + h + H, pl.ds(H, E)] = blocks[h * E : (h + 1) * E]

    def side(at):
        return 0 if at == 0 else 2 if at == E + 1 else 1

    def put_first(x, y, value):
        first[x, y] = (value * mask_ref[side(x), side(y)]).astype(jnp.bfloat16)

    def put_second(x, y, value):
        second[x, y] = (value * mask).astype(jnp.bfloat16)

    def one(x, y):
        conv_pair(grid, w1, bias_ref[0], ((x, y), (x, y + 1)), put_first)

    def two(x, y):
        conv_pair(first, w2, bias_ref[1], ((x, y), (x, y + 1)), put_second)

    def lower(k):
        x = 2 * k
        slab_ref[k] = jnp.swapaxes(jnp.concatenate([second[x], second[x + 1]], axis=0), 0, 1)
        stacked = []
        for a in range(2):
            for b in range(2):
                stacked.append(jnp.concatenate([second[x + a, y + b] for y in range(0, E, 2)], axis=1))
        sums = jnp.dot(wd[...], jnp.concatenate(stacked, axis=0), preferred_element_type=jnp.float32)
        lowered = []
        for y in range(E // 2):
            part = sums[:, y * Z : (y + 1) * Z]
            value = part[:C] + pltpu.roll(part[C:], Z - 1, 1) + bias_ref[2]
            lowered.append(jnp.maximum(value, 0.0).astype(jnp.bfloat16))
        return lowered

    def thin(planes):
        rows = []
        for _, lowered in planes:
            for h in range(2):
                rows.append(jnp.concatenate(lowered[2 * h : 2 * h + 2], axis=1))
        if not rows:
            return
        kept = jnp.dot(jnp.concatenate(rows, axis=0), keep[...], preferred_element_type=jnp.float32)
        for i, (k, _) in enumerate(planes):
            for h in range(2):
                at = (2 * i + h) * C
                narrow[h, pl.ds(k, C, stride=E // 2), :] = kept[at : at + C]

    pl.semaphore_wait(barrier, count)
    for name in SENDS:
        start(groups[name])

    for dr, dd in CORNERS + FACES_X + FACES_Y:

        @pl.when(jnp.logical_not(there(-dr, -dd)))
        def _():
            nx, ny = (E if dr == 0 else H), (E if dd == 0 else H)
            grid[landing_span(dr), landing_span(dd)] = jnp.zeros((nx, ny, C, Z), jnp.bfloat16)

    loads[1].wait()
    prepare_weight(w_held.at[0], w1)
    for k in range(3):
        loads[4 + k].wait()
        bias_ref[k] = jnp.broadcast_to(column(b_held[k]), (C, Z))
    for x in range(2, E):
        for y in range(2, E, 2):
            one(x, y)
    loads[2].wait()
    prepare_weight(w_held.at[1], w2)
    loads[3].wait()
    wide[...] = wd_held[...].astype(jnp.float32)
    for c in range(2):
        for a in range(2):
            both = [wide[pl.ds(a * 4 + b * 2 + c, C, stride=8), :].astype(jnp.bfloat16) for b in range(2)]
            wd[pl.ds(c * C, C), pl.ds(a * 2 * C, 2 * C)] = jnp.concatenate(both, axis=1)
    lane_in = lax.broadcasted_iota(jnp.int32, (2 * Z, Z), 0)
    lane_out = lax.broadcasted_iota(jnp.int32, (2 * Z, Z), 1)
    keep[...] = jnp.where(lane_in == 2 * lane_out, 1.0, 0.0).astype(jnp.bfloat16)

    for x in range(2, E - 2):
        for y in range(2, E - 2, 2):
            two(x, y)

    landed, landed_rim = set(range(H, E + H)), set()
    one_middle, one_rim = set(range(2, E)), set()
    two_middle, two_rim = set(range(2, E - 2)), set()

    complete = []

    def advance(last):
        lowered = [(k, lower(k)) for k in complete]
        complete.clear()
        for x in range(E + 2):
            if x not in one_middle and {x, x + 1, x + 2} <= landed:
                for y in range(2, E, 2):
                    one(x, y)
                one_middle.add(x)
        for x in range(E + 2):
            if x not in one_rim and {x, x + 1, x + 2} <= landed_rim:
                for y in (0, E):
                    one(x, y)
                one_rim.add(x)
        thin(lowered)
        for x in range(E):
            if x not in two_middle and {x, x + 1, x + 2} <= one_middle:
                for y in range(2, E - 2, 2):
                    two(x, y)
                two_middle.add(x)
        for x in range(E):
            if x not in two_rim and {x, x + 1, x + 2} <= one_rim & one_middle:
                for y in (0, E - 2):
                    two(x, y)
                two_rim.add(x)
                if x ^ 1 in two_rim:
                    complete.append(x // 2)
        if last:
            thin([(k, lower(k)) for k in complete])

    for name in TAKES:
        arrived(groups[name])
        if name == "near":
            landed.update((1, E + H))
        elif name == "far":
            landed.update((0, E + H + 1))
        elif name == "low":
            landed_rim.update(range(H))
        elif name == "high":
            landed_rim.update(range(E + H, E + 2 * H))
        else:
            first_x, planes_x = CHUNKS[int(name)]
            landed_rim.update(range(H + first_x, H + first_x + planes_x))
            if first_x == 0:
                start(groups["high"])
        if name != "3":
            advance(name == TAKES[-1])
    for k in range(2):
        down_ref[:, :, pl.ds(k * Z, Z)] = narrow[k].reshape(C, E // 2, Z).astype(jnp.bfloat16)
    for copy, goes, _ in made:
        pl.when(goes)(copy.wait_send)


def local_kernel(slab_ref, down_in, skip_hbm, down_hbm, copy_sem):
    copies = [pltpu.make_async_copy(down_in, down_hbm, copy_sem.at[E // 2])]
    for k in range(E // 2):
        copies.append(pltpu.make_async_copy(slab_ref.at[k], skip_hbm.at[:, pl.ds(2 * k * E, 2 * E), :], copy_sem.at[k]))
    for copy in copies:
        copy.start()
    for copy in copies:
        copy.wait()


def on_device(shape, features, occupancy, weight_one, bias_one, weight_two, bias_two, weight_down, bias_down):
    bf16, f32 = jnp.bfloat16, jnp.float32
    hbm = pl.BlockSpec(memory_space=pltpu.HBM)
    vmem = pl.BlockSpec(memory_space=pltpu.VMEM)
    held = [w.transpose(2, 3, 4, 0, 1).reshape(27, C, C) for w in (weight_one, weight_two)]
    n_copies = 2 * len(CHUNKS) + 8
    n_loads = 7 + E // 2
    operands = (
        features.reshape(C, E * E, Z),
        occupancy.transpose(0, 2, 1),
        held[0],
        bias_one.reshape(1, C),
        held[1],
        bias_two.reshape(1, C),
        weight_down.transpose(0, 2, 3, 4, 1).reshape(8 * C, C),
        bias_down.reshape(1, C),
    )
    slabs, down = pl.pallas_call(
        functools.partial(remote_kernel, shape),
        out_shape=(
            jax.ShapeDtypeStruct((E // 2, C, 2 * E, Z), bf16),
            jax.ShapeDtypeStruct((C, E // 2, 2 * Z), bf16),
        ),
        in_specs=[hbm] * len(operands),
        out_specs=(vmem, vmem),
        scratch_shapes=[
            pltpu.VMEM((E // 2, C, 2 * E, Z), bf16),
            pltpu.VMEM((shape[0], occupancy.shape[2], shape[1]), jnp.int32),
            pltpu.VMEM((3, 1, C), f32),
            pltpu.VMEM((E + 2 * H, E + 2 * H, C, Z), bf16),
            pltpu.VMEM((E + 2, E + 2, C, Z), bf16),
            pltpu.VMEM((E, E, C, Z), bf16),
            pltpu.VMEM((2, 27, C, C), bf16),
            pltpu.VMEM((3 * C, TAPS * C), bf16),
            pltpu.VMEM((3 * C, TAPS * C), bf16),
            pltpu.VMEM((8 * C, C), bf16),
            pltpu.VMEM((8 * C, C), f32),
            pltpu.VMEM((2 * C, 4 * C), bf16),
            pltpu.VMEM((2 * Z, Z), bf16),
            pltpu.VMEM((2, C * E // 2, Z), f32),
            pltpu.VMEM((3, 3, 1, Z), f32),
            pltpu.VMEM((3, C, Z), f32),
            pltpu.SemaphoreType.DMA((n_loads,)),
            pltpu.SemaphoreType.DMA((n_copies,)),
            pltpu.SemaphoreType.DMA((n_copies,)),
        ],
        compiler_params=pltpu.CompilerParams(
            collective_id=0, has_side_effects=True, vmem_limit_bytes=32 * 1024 * 1024
        ),
        name="halo_convs",
    )(*(pltpu.with_memory_space_constraint(operand, pltpu.HBM) for operand in operands))
    skip, down = pl.pallas_call(
        local_kernel,
        out_shape=(
            jax.ShapeDtypeStruct((C, E * E, Z), bf16),
            jax.ShapeDtypeStruct((C, E // 2, 2 * Z), bf16),
        ),
        in_specs=[vmem] * 2,
        out_specs=(hbm, hbm),
        scratch_shapes=[pltpu.SemaphoreType.DMA((E // 2 + 1,))],
        compiler_params=pltpu.CompilerParams(vmem_limit_bytes=32 * 1024 * 1024),
        name="copy_out",
    )(slabs, down)
    return skip.reshape(C, E, E, Z), down


def solution(mesh):
    return jax.shard_map(
        functools.partial(on_device, (mesh.shape["region"], mesh.shape["dev"])),
        mesh=mesh,
        in_specs=(P(None, "region", "dev", None), P(), P(), P(), P(), P(), P(), P()),
        out_specs=(P(None, "region", "dev", None), P(None, "region", "dev")),
        check_vma=False,
    )
```

```python
import functools

import jax
import jax.numpy as jnp
from jax import lax
from jax.experimental import pallas as pl
from jax.experimental.pallas import tpu as pltpu
from jax.sharding import PartitionSpec as P

MESH = pl.DeviceIdType.MESH
FACES_X = ((1, 0), (-1, 0))
FACES_Y = ((0, 1), (0, -1))
CORNERS = ((1, 1), (1, -1), (-1, 1), (-1, -1))
DIRECT, PASSED = CORNERS[:2], CORNERS[2:]
E = 8
H = 2
C = 64
Z = 128
TAPS = 9
CHUNKS = ((0, 2), (2, 2), (4, 2), (6, 2))
SLABS = (0, 3, 1, 2)
SENDS = ("0", "near", "low", "far", "1", "2", "3")
TAKES = ("0", "near", "far", "low", "1", "2", "3", "high")


def source_span(step):
    return pl.ds(H, E) if step == 0 else pl.ds(E if step > 0 else H, H)


def landing_span(step):
    return pl.ds(H, E) if step == 0 else pl.ds(0 if step > 0 else E + H, H)


def column(row):
    spread = jnp.broadcast_to(row, (C, C))
    on_diagonal = lax.broadcasted_iota(jnp.int32, (C, C), 0) == lax.broadcasted_iota(jnp.int32, (C, C), 1)
    return jnp.sum(jnp.where(on_diagonal, spread, 0.0), axis=1, keepdims=True)


def prepare_weight(held, ready):
    for c in range(3):
        rows = pl.ds(c * C, C)
        for pair in range(TAPS // 2):
            both = jnp.concatenate([held[(2 * pair) * 3 + c], held[(2 * pair + 1) * 3 + c]], axis=1)
            ready[rows, pl.ds(pair * 2 * C, 2 * C)] = both
        ready[rows, pl.ds((TAPS - 1) * C, C)] = held[(TAPS - 1) * 3 + c]


def conv_pair(src, ready, bias, spots, put):
    stacked = []
    for a in range(3):
        for b in range(3):
            stacked.append(jnp.concatenate([src[x + a, y + b] for x, y in spots], axis=1))
    sums = jnp.dot(ready[...], jnp.concatenate(stacked, axis=0), preferred_element_type=jnp.float32)
    lane = lax.broadcasted_iota(jnp.int32, (C, Z), 1)
    for half, (x, y) in enumerate(spots):
        part = sums[:, half * Z : (half + 1) * Z]
        before = jnp.where(lane == 0, 0.0, pltpu.roll(part[:C], 1, 1))
        after = jnp.where(lane == Z - 1, 0.0, pltpu.roll(part[2 * C :], Z - 1, 1))
        put(x, y, jnp.maximum(part[C : 2 * C] + before + after + bias, 0.0))


def remote_kernel(
    shape, feat_hbm, occ_hbm, w1_hbm, b1_hbm, w2_hbm, b2_hbm, wd_hbm, bd_hbm, slab_ref, down_ref,
    feat, occ_ref, b_held, grid, first, second, w_held, w1, w2, wd_held, wide, wd, keep, narrow, mask_ref, bias_ref,
    copy_sem, send_sem, recv_sem,
):
    n_region, n_dev = shape
    region, dev = lax.axis_index("region"), lax.axis_index("dev")
    pairs = (
        (occ_hbm, occ_ref),
        (w1_hbm, w_held.at[0]),
        (w2_hbm, w_held.at[1]),
        (wd_hbm, wd_held),
        (b1_hbm, b_held.at[0]),
        (b2_hbm, b_held.at[1]),
        (bd_hbm, b_held.at[2]),
    )
    planes = []
    for k in range(E // 2):
        part = feat_hbm.at[:, pl.ds(2 * k * E, 2 * E), :]
        planes.append(pltpu.make_async_copy(part, feat.at[k], copy_sem.at[len(pairs) + k]))
    loads = [pltpu.make_async_copy(src, dst, copy_sem.at[k]) for k, (src, dst) in enumerate(pairs)]
    loads[0].start()
    for k in SLABS:
        planes[k].start()
    for load in loads[1:]:
        load.start()

    def there(dr, dd):
        r, d = region + dr, dev + dd
        return (r >= 0) & (r < n_region) & (d >= 0) & (d < n_dev)

    barrier = pltpu.get_barrier_semaphore()
    count = 0
    for dr, dd in FACES_Y + FACES_X + DIRECT:
        count = count + there(dr, dd).astype(jnp.int32)

        @pl.when(there(-dr, -dd))
        def _():
            pl.semaphore_signal(barrier, inc=1, device_id=(region - dr, dev - dd), device_id_type=MESH)

    made = []

    def transfer(to, src, dst, goes, comes):
        copy = pltpu.make_async_remote_copy(
            src_ref=grid.at[src],
            dst_ref=grid.at[dst],
            send_sem=send_sem.at[len(made)],
            recv_sem=recv_sem.at[len(made)],
            device_id=(region + to[0], dev + to[1]),
            device_id_type=MESH,
        )
        made.append((copy, goes, comes))
        return made[-1]

    def straight(dr, dd):
        src, dst = (source_span(dr), source_span(dd)), (landing_span(dr), landing_span(dd))
        return transfer((dr, dd), src, dst, there(dr, dd), there(-dr, -dd))

    def passed_on(dr, dd):
        src, dst = (source_span(dr), landing_span(dd)), (landing_span(dr), landing_span(dd))
        return transfer((dr, 0), src, dst, there(dr, 0) & there(dr, -dd) & there(0, -dd), there(-dr, -dd))

    groups = {"low": [straight(*way) for way in DIRECT], "high": [passed_on(*way) for way in PASSED]}
    for name, up, down in (("near", (E + 1, 1), (H, E + H)), ("far", (E, 0), (H + 1, E + H + 1))):
        groups[name] = []
        for dr, (src, dst) in ((1, up), (-1, down)):
            src, dst = (pl.ds(src, 1), pl.ds(H, E)), (pl.ds(dst, 1), pl.ds(H, E))
            groups[name].append(transfer((dr, 0), src, dst, there(dr, 0), there(-dr, 0)))
    for k, (first_x, planes_x) in enumerate(CHUNKS):
        groups[str(k)] = []
        x = pl.ds(H + first_x, planes_x)
        for dr, dd in FACES_Y:
            src, dst = (x, source_span(dd)), (x, landing_span(dd))
            groups[str(k)].append(transfer((dr, dd), src, dst, there(dr, dd), there(-dr, -dd)))

    def start(group):
        for copy, goes, _ in group:
            pl.when(goes)(copy.start)

    def arrived(group):
        for copy, _, comes in group:
            pl.when(comes)(copy.wait_recv)

    loads[0].wait()
    bricks, devs = occ_ref.shape[1:]
    lanes = lax.broadcasted_iota(jnp.int32, (bricks, devs), 1)
    brick = lax.broadcasted_iota(jnp.int32, (bricks, Z), 0)
    voxel = lax.broadcasted_iota(jnp.int32, (bricks, Z), 1)
    span = Z // bricks
    inside = (voxel >= brick * span) & (voxel < (brick + 1) * span)
    for dr in (-1, 0, 1):
        valid = (region + dr >= 0) & (region + dr < n_region)
        held = occ_ref[jnp.clip(region + dr, 0, n_region - 1)].astype(jnp.float32)
        held = held * valid.astype(jnp.float32)
        for dd in (-1, 0, 1):
            level = jnp.sum(jnp.where(lanes == dev + dd, held, 0.0), axis=1, keepdims=True)
            mask_ref[dr + 1, dd + 1] = jnp.sum(jnp.where(inside, level, 0.0), axis=0, keepdims=True)

    mask = mask_ref[1, 1]
    for k in SLABS:
        planes[k].wait()
        blocks = jnp.swapaxes(feat[k], 0, 1)
        blocks = jnp.where(mask[None] > 0, blocks, jnp.zeros_like(blocks))
        for h in range(2):
            grid[2 * k + h + H, pl.ds(H, E)] = blocks[h * E : (h + 1) * E]

    def side(at):
        return 0 if at == 0 else 2 if at == E + 1 else 1

    def put_first(x, y, value):
        first[x, y] = (value * mask_ref[side(x), side(y)]).astype(jnp.bfloat16)

    def put_second(x, y, value):
        second[x, y] = (value * mask).astype(jnp.bfloat16)

    def one(x, y):
        conv_pair(grid, w1, bias_ref[0], ((x, y), (x, y + 1)), put_first)

    def two(x, y):
        conv_pair(first, w2, bias_ref[1], ((x, y), (x, y + 1)), put_second)

    def lower(k):
        x = 2 * k
        slab_ref[k] = jnp.swapaxes(jnp.concatenate([second[x], second[x + 1]], axis=0), 0, 1)
        stacked = []
        for a in range(2):
            for b in range(2):
                stacked.append(jnp.concatenate([second[x + a, y + b] for y in range(0, E, 2)], axis=1))
        sums = jnp.dot(wd[...], jnp.concatenate(stacked, axis=0), preferred_element_type=jnp.float32)
        lowered = []
        for y in range(E // 2):
            part = sums[:, y * Z : (y + 1) * Z]
            value = part[:C] + pltpu.roll(part[C:], Z - 1, 1) + bias_ref[2]
            lowered.append(jnp.maximum(value, 0.0).astype(jnp.bfloat16))
        return lowered

    def thin(planes):
        rows = []
        for _, lowered in planes:
            for h in range(2):
                rows.append(jnp.concatenate(lowered[2 * h : 2 * h + 2], axis=1))
        if not rows:
            return
        kept = jnp.dot(jnp.concatenate(rows, axis=0), keep[...], preferred_element_type=jnp.float32)
        for i, (k, _) in enumerate(planes):
            for h in range(2):
                at = (2 * i + h) * C
                narrow[h, pl.ds(k, C, stride=E // 2), :] = kept[at : at + C]

    pl.semaphore_wait(barrier, count)
    for name in SENDS:
        start(groups[name])

    for dr, dd in CORNERS + FACES_X + FACES_Y:

        @pl.when(jnp.logical_not(there(-dr, -dd)))
        def _():
            nx, ny = (E if dr == 0 else H), (E if dd == 0 else H)
            grid[landing_span(dr), landing_span(dd)] = jnp.zeros((nx, ny, C, Z), jnp.bfloat16)

    loads[1].wait()
    prepare_weight(w_held.at[0], w1)
    for k in range(3):
        loads[4 + k].wait()
        bias_ref[k] = jnp.broadcast_to(column(b_held[k]), (C, Z))
    for x in range(2, E):
        for y in range(2, E, 2):
            one(x, y)
    loads[2].wait()
    prepare_weight(w_held.at[1], w2)
    loads[3].wait()
    wide[pl.ds(0, 8 * C), :] = wd_held[...].astype(jnp.float32)
    for c in range(2):
        for a in range(2):
            both = [wide[pl.ds(a * 4 + b * 2 + c, C, stride=8), :].astype(jnp.bfloat16) for b in range(2)]
            wd[pl.ds(c * C, C), pl.ds(a * 2 * C, 2 * C)] = jnp.concatenate(both, axis=1)
    lane_in = lax.broadcasted_iota(jnp.int32, (2 * Z, Z), 0)
    lane_out = lax.broadcasted_iota(jnp.int32, (2 * Z, Z), 1)
    keep[...] = jnp.where(lane_in == 2 * lane_out, 1.0, 0.0).astype(jnp.bfloat16)

    for x in range(2, E - 2):
        for y in range(2, E - 2, 2):
            two(x, y)

    landed, landed_rim = set(range(H, E + H)), set()
    one_middle, one_rim = set(range(2, E)), set()
    two_middle, two_rim = set(range(2, E - 2)), set()

    complete = []

    def advance(last):
        lowered = [(k, lower(k)) for k in complete]
        complete.clear()
        for x in range(E + 2):
            if x not in one_middle and {x, x + 1, x + 2} <= landed:
                for y in range(2, E, 2):
                    one(x, y)
                one_middle.add(x)
        for x in range(E + 2):
            if x not in one_rim and {x, x + 1, x + 2} <= landed_rim:
                for y in (0, E):
                    one(x, y)
                one_rim.add(x)
        thin(lowered)
        for x in range(E):
            if x not in two_middle and {x, x + 1, x + 2} <= one_middle:
                for y in range(2, E - 2, 2):
                    two(x, y)
                two_middle.add(x)
        for x in range(E):
            if x not in two_rim and {x, x + 1, x + 2} <= one_rim & one_middle:
                for y in (0, E - 2):
                    two(x, y)
                two_rim.add(x)
                if x ^ 1 in two_rim:
                    complete.append(x // 2)
        if last:
            thin([(k, lower(k)) for k in complete])

    for name in TAKES:
        arrived(groups[name])
        if name == "near":
            landed.update((1, E + H))
        elif name == "far":
            landed.update((0, E + H + 1))
        elif name == "low":
            landed_rim.update(range(H))
        elif name == "high":
            landed_rim.update(range(E + H, E + 2 * H))
        else:
            first_x, planes_x = CHUNKS[int(name)]
            landed_rim.update(range(H + first_x, H + first_x + planes_x))
            if first_x == 0:
                start(groups["high"])
        if name != "3":
            advance(name == TAKES[-1])
    for k in range(2):
        down_ref[:, :, pl.ds(k * Z, Z)] = narrow[k, pl.ds(0, C * E // 2), :].reshape(C, E // 2, Z).astype(jnp.bfloat16)
    for copy, goes, _ in made:
        pl.when(goes)(copy.wait_send)


def local_kernel(slab_ref, down_in, skip_hbm, down_hbm, copy_sem):
    copies = [pltpu.make_async_copy(down_in, down_hbm, copy_sem.at[E // 2])]
    for k in range(E // 2):
        copies.append(pltpu.make_async_copy(slab_ref.at[k], skip_hbm.at[:, pl.ds(2 * k * E, 2 * E), :], copy_sem.at[k]))
    for copy in copies:
        copy.start()
    for copy in copies:
        copy.wait()


def on_device(shape, features, occupancy, weight_one, bias_one, weight_two, bias_two, weight_down, bias_down):
    bf16, f32 = jnp.bfloat16, jnp.float32
    hbm = pl.BlockSpec(memory_space=pltpu.HBM)
    vmem = pl.BlockSpec(memory_space=pltpu.VMEM)
    held = [w.transpose(2, 3, 4, 0, 1).reshape(27, C, C) for w in (weight_one, weight_two)]
    n_copies = 2 * len(CHUNKS) + 8
    n_loads = 7 + E // 2
    operands = (
        features.reshape(C, E * E, Z),
        occupancy.transpose(0, 2, 1),
        held[0],
        bias_one.reshape(1, C),
        held[1],
        bias_two.reshape(1, C),
        weight_down.transpose(0, 2, 3, 4, 1).reshape(8 * C, C),
        bias_down.reshape(1, C),
    )
    slabs, down = pl.pallas_call(
        functools.partial(remote_kernel, shape),
        out_shape=(
            jax.ShapeDtypeStruct((E // 2, C, 2 * E, Z), bf16),
            jax.ShapeDtypeStruct((C, E // 2, 2 * Z), bf16),
        ),
        in_specs=[hbm] * len(operands),
        out_specs=(vmem, vmem),
        scratch_shapes=[
            pltpu.VMEM((E // 2, C, 2 * E, Z), bf16),
            pltpu.VMEM((shape[0], occupancy.shape[2], shape[1]), jnp.int32),
            pltpu.VMEM((3, 1, C), f32),
            pltpu.VMEM((E + 2 * H, E + 2 * H, C, Z), bf16),
            pltpu.VMEM((E + 2, E + 2, C, Z), bf16),
            pltpu.VMEM((E, E, C, Z), bf16),
            pltpu.VMEM((2, 27, C, C), bf16),
            pltpu.VMEM((3 * C, TAPS * C), bf16),
            pltpu.VMEM((3 * C, TAPS * C), bf16),
            pltpu.VMEM((8 * C, C), bf16),
            pltpu.VMEM((8 * C + 8, C), f32),
            pltpu.VMEM((2 * C, 4 * C), bf16),
            pltpu.VMEM((2 * Z, Z), bf16),
            pltpu.VMEM((2, C * E // 2 + 8, Z), f32),
            pltpu.VMEM((3, 3, 1, Z), f32),
            pltpu.VMEM((3, C, Z), f32),
            pltpu.SemaphoreType.DMA((n_loads,)),
            pltpu.SemaphoreType.DMA((n_copies,)),
            pltpu.SemaphoreType.DMA((n_copies,)),
        ],
        compiler_params=pltpu.CompilerParams(
            collective_id=0, has_side_effects=True, vmem_limit_bytes=32 * 1024 * 1024
        ),
        name="halo_convs",
    )(*(pltpu.with_memory_space_constraint(operand, pltpu.HBM) for operand in operands))
    skip, down = pl.pallas_call(
        local_kernel,
        out_shape=(
            jax.ShapeDtypeStruct((C, E * E, Z), bf16),
            jax.ShapeDtypeStruct((C, E // 2, 2 * Z), bf16),
        ),
        in_specs=[vmem] * 2,
        out_specs=(hbm, hbm),
        scratch_shapes=[pltpu.SemaphoreType.DMA((E // 2 + 1,))],
        compiler_params=pltpu.CompilerParams(vmem_limit_bytes=32 * 1024 * 1024),
        name="copy_out",
    )(slabs, down)
    return skip.reshape(C, E, E, Z), down


def solution(mesh):
    return jax.shard_map(
        functools.partial(on_device, (mesh.shape["region"], mesh.shape["dev"])),
        mesh=mesh,
        in_specs=(P(None, "region", "dev", None), P(), P(), P(), P(), P(), P(), P()),
        out_specs=(P(None, "region", "dev", None), P(None, "region", "dev")),
        check_vma=False,
    )
```
